32 devices in a mesh: dp: 4 (over z), expert: 8 (over y, x, core).
Axes of the slice: x: 2, y: 2, z: 4, core: 2. Of those that a mesh axis runs over, the one named last changes fastest.
Arguments:
- tokens: bfloat16 [4096, 1024], P(('dp', 'expert')), may hold values from -6 to 6
- cotangent: bfloat16 [4096, 1024], P(('dp', 'expert')), may hold values from -6 to 6
- expert_ids: int32 [4096, 8], P(('dp', 'expert')), may hold values from 0 to 15, all different within a row; in each aligned block of 128 rows (0 to 127, 128 to 255, ...) at most 80 rows name the same one
- route_weights: float32 [4096, 8], P(('dp', 'expert')), may hold values from 0.05 to 0.25
- weight_in: bfloat16 [1024, 16, 768], P('dp', 'expert'), may hold values from -0.1875 to 0.1875
- weight_down: bfloat16 [384, 16, 1024], P('dp', 'expert'), may hold values from -0.3125 to 0.3125
Outputs:
- token_grad: bfloat16 [4096, 1024], P(('dp', 'expert'))
- grad_in: bfloat16 [1024, 16, 768], P('dp', 'expert')
The draws below stay inside these ranges and needn't reach their ends.
Inputs may be any that keep to these rules, and one draw needn't show every extreme that they name: `expert_ids`: each token names 8 different experts. Among the 128 tokens of one device at most 80 name the same expert, a bound that some block reaches.
All inputs are finite; a program needn't handle non-finite values.
Results may differ from the reference program's by a relative error of at most 0.018.
Values may be sent and summed in bfloat16 or wider, within the bound.
No kernel may reach another device: no remote copies, remote signals or barrier semaphores. Data moves between devices by JAX's collectives and lax.ppermute only.
A program may use at most 64 MiB of HBM per device.

```python
import math
import jax
import jax.numpy as jnp
import numpy as np
from jax import lax

D = 1024
FF = 384
TOPK = 8
TOK_DEV = 128
EXPERTS = 16
CAP = 80
ROWS_EXP = 2048
TOKENS = 4096
N_DP = 4
N_EXPERT = 8


def spiked(array, rng, source, target, parts, factor):
    def block_of(dim):
        return (jnp.arange(array.shape[dim]) // (array.shape[dim] // parts)).reshape((-1,) + (1,) * (array.ndim - 1 - dim))

    first = jax.random.permutation(rng, parts)[block_of(target)]
    other_side = (block_of(target) + parts // 2) % parts
    return jnp.where((block_of(source) == first) | (block_of(source) == other_side), factor * array, array)


def levels(rng, shape, pieces, smallest, largest):
    def one(axis_at, parts):
        steps = jax.random.uniform(jax.random.fold_in(jax.random.fold_in(rng, 6), axis_at), (parts,), jnp.float32, smallest / len(pieces), largest / len(pieces))
        return jnp.repeat(jnp.exp(steps), shape[axis_at] // parts).reshape((-1,) + (1,) * (len(shape) - axis_at - 1))

    gain = one(*pieces[0])
    for cut in pieces[1:]:
        gain = gain * one(*cut)
    return gain


def shared_out(rng, own, number, rows, count, top, reach, lean):
    ranking = jax.random.permutation(rng, count)
    crowded, ordinary = shares(count, rows * top, reach, lean, True), shares(count, rows * top, reach, lean, False)
    places = jnp.arange(count)

    def named(tallies, offset_by):
        used = int((tallies > 0).sum())
        fixed = max(1, used // 4)
        moved = fixed + (places - fixed + offset_by * (used - fixed)) % max(1, count - fixed)
        return jnp.zeros((count,), jnp.int32).at[ranking[jnp.where(places < fixed, places, moved)]].set(jnp.asarray(tallies, jnp.int32))

    tallies = jnp.where(number % 4 == 0, named(crowded, number // 4), named(ordinary, number - number // 4 - 1))
    mixed = jax.random.permutation(jax.random.fold_in(own, 3), count)
    source_of, taker = mixed[0:count // 2 * 2:2], mixed[1:count // 2 * 2:2]
    room = jnp.minimum(tallies[source_of] - 1, reach - tallies[taker]) // 2
    room = jnp.where((source_of == ranking[0]) | (taker == ranking[0]) | (tallies[taker] == 0), 0, jnp.maximum(room, 0))
    moved = jax.random.randint(jax.random.fold_in(own, 4), (count // 2,), 0, 1 << 20) % (room + 1)
    tallies = tallies.at[source_of].add(-moved).at[taker].add(moved)
    items = jnp.searchsorted(jnp.cumsum(tallies), jnp.arange(rows * top), side="right").astype(jnp.int32)
    table = items.reshape(top, rows).T
    table = table[jax.random.permutation(jax.random.fold_in(own, 1), rows)]
    offset_by = jax.random.randint(jax.random.fold_in(own, 2), (rows, 1), 0, top)
    return jnp.take_along_axis(table, (jnp.arange(top)[None, :] + offset_by) % top, axis=1)


def shares(number_of, total, most, skew, full):
    loads = [(1 << 20) // math.isqrt(standing ** skew) + 1 for standing in range(1, number_of + 1)]
    largest = most if full else min(most, max(-(-total // number_of), total * loads[0] // sum(loads)))
    least = 1 if total - largest >= number_of - 1 else 0
    holding, spare = [largest] + [least] * (number_of - 1), total - largest - least * (number_of - 1)
    while spare > 0:
        free = [i for i in range(1, number_of) if holding[i] < largest] or [i for i in range(1, number_of) if holding[i] < most]
        pool, remaining = sum([loads[i] for i in free]), spare
        for i in free:
            more = min(most - holding[i], max(1, remaining * loads[i] // pool), spare)
            holding[i] = holding[i] + more
            spare = spare - more
    return np.array(holding)


def centred(own_key, dims, deviation, limit, shards=(), kind=jnp.bfloat16):
    result = deviation * jax.random.normal(own_key, dims, jnp.float32)
    if shards:
        result = result * levels(own_key, dims, shards, -0.22, 0.18)
    return jnp.clip(result, -limit, limit).astype(kind)


def heavy_noise(own_key, dims, scale, reach, shards, heavy, held_as=jnp.bfloat16):
    drawn = scale * jax.random.normal(own_key, dims, jnp.float32)
    if shards:
        drawn = drawn * levels(own_key, dims, shards, -0.22, 0.18)
    return jnp.clip(spiked(drawn, jax.random.fold_in(own_key, 3), *heavy), -reach, reach).astype(held_as)


def setup_inputs(seed: int = 0) -> dict:
    key_of = jax.random.split(jax.random.key(seed), 7)
    tokens = heavy_noise(key_of[0], (TOKENS, D), 1.0, 6.0, ((0, 32),), (0, 1, 32, 2.75))
    cotangent = centred(key_of[1], (TOKENS, D), 1.0, 6.0, ((0, 32),))
    expert_ids_keys = jax.random.split(jax.random.fold_in(key_of[2], 1), TOKENS // TOK_DEV)
    expert_ids_turns = jax.random.permutation(jax.random.fold_in(key_of[2], 3), TOKENS // TOK_DEV)
    expert_ids = jax.vmap(lambda own, number: shared_out(jax.random.fold_in(key_of[2], 2), own, number, TOK_DEV, EXPERTS, TOPK, CAP, 1))(expert_ids_keys, expert_ids_turns).reshape((TOKENS, TOPK))
    route_weights = jnp.clip(0.05 + 0.2 * jax.random.uniform(key_of[3], (TOKENS, TOPK), jnp.float32) ** levels(key_of[3], (TOKENS, TOPK), ((0, 32),), -0.2, 0.2), 0.05, 0.25)
    weight_in = centred(key_of[4], (D, EXPERTS, 2 * FF), D ** -0.5, 0.1875, ((0, 4), (1, 8)))
    weight_down = centred(key_of[5], (FF, EXPERTS, D), FF ** -0.5, 0.3125, ((0, 4), (1, 8)))
    return {"tokens": tokens, "cotangent": cotangent, "expert_ids": expert_ids, "route_weights": route_weights, "weight_in": weight_in, "weight_down": weight_down}


def reference(tokens, cotangent, expert_ids, route_weights, weight_in, weight_down):
    devices = N_DP * N_EXPERT
    per_device = TOK_DEV * TOPK
    id_rows = expert_ids.reshape(devices, per_device)
    one_hot = (id_rows[:, :, None] == jnp.arange(EXPERTS, dtype=jnp.int32)[None, None, :]).astype(jnp.int32)
    ranks = jnp.cumsum(one_hot, axis=1) - 1
    slots = jnp.sum(ranks * one_hot, axis=2).astype(jnp.int32)
    owner = jnp.arange(devices, dtype=jnp.int32)[:, None]
    target = ((owner * EXPERTS + id_rows) * CAP + slots).reshape(-1).astype(jnp.int32)
    routes = jnp.arange(devices * per_device, dtype=jnp.int32)
    table = jnp.full((devices * EXPERTS * CAP,), TOKENS * TOPK, jnp.int32).at[target].set(routes)
    table = table.reshape(devices, EXPERTS, CAP)
    blank = jnp.zeros((1, D), jnp.bfloat16)
    padded_tokens = jnp.concatenate([tokens, blank], 0)
    padded_grads = jnp.concatenate([cotangent, blank], 0)
    padded_weights = jnp.concatenate([route_weights.reshape(-1), jnp.zeros((1,), jnp.float32)], 0)
    grad_scale = float(ROWS_EXP) ** -0.5

    def one_expert(accum, expert):
        index = lax.dynamic_index_in_dim(table, expert, 1, keepdims=False).reshape(-1).astype(jnp.int32)
        source = (index // TOPK).astype(jnp.int32)
        rows_tokens = padded_tokens[source]
        rows_grads = padded_grads[source]
        weights_here = padded_weights[index]
        proj_in = lax.dynamic_index_in_dim(weight_in, expert, 1, keepdims=False)
        proj_down = lax.dynamic_index_in_dim(weight_down, expert, 1, keepdims=False)
        gate_up = jnp.dot(rows_tokens, proj_in, preferred_element_type=jnp.float32)
        gate = gate_up[:, :FF]
        upper = gate_up[:, FF:]
        hidden_grad = jnp.dot(rows_grads, proj_down.T, preferred_element_type=jnp.float32)
        sigma = jax.nn.sigmoid(gate)
        grad_gate = hidden_grad * upper * sigma * (1.0 + gate * (1.0 - sigma))
        grad_up = hidden_grad * gate * sigma
        grad_mid = jnp.concatenate([grad_gate, grad_up], 1).astype(jnp.bfloat16)
        input_part = jnp.dot(grad_mid, proj_in.T, preferred_element_type=jnp.float32).astype(jnp.bfloat16)
        input_part = lax.optimization_barrier(input_part)
        contrib = weights_here[:, None] * input_part.astype(jnp.float32)
        accum = accum.at[source].add(contrib)
        grouped_tokens = rows_tokens.reshape(N_DP, N_EXPERT * CAP, D).astype(jnp.float32)
        grouped_mid = grad_mid.reshape(N_DP, N_EXPERT * CAP, 2 * FF).astype(jnp.float32)
        partial_sums = jnp.einsum("qrd,qri->qdi", grouped_tokens, grouped_mid) * grad_scale
        partial_sums = lax.optimization_barrier(partial_sums.astype(jnp.bfloat16))
        grad_expert = jnp.sum(partial_sums.astype(jnp.float32), axis=0).astype(jnp.bfloat16)
        return accum, grad_expert

    accum, grads = lax.scan(one_expert, jnp.zeros((TOKENS + 1, D), jnp.float32), jnp.arange(EXPERTS, dtype=jnp.int32))
    token_grad = accum[:TOKENS].astype(jnp.bfloat16)
    grad_in = jnp.transpose(grads, (1, 0, 2))
    return token_grad, grad_in
```

```python
import functools

import jax
import jax.numpy as jnp
from jax import lax
from jax.experimental import pallas as pl
from jax.experimental.pallas import tpu as pltpu
from jax.sharding import PartitionSpec as P


def by_routes(tokens, cotangent, expert_ids, route_weights, weight_in, weight_down):
    token_count = tokens.shape[0]
    width = tokens.shape[1]
    route_count = expert_ids.shape[1]
    peers = lax.axis_size("expert")
    local_experts = weight_in.shape[1]
    experts = local_experts * peers
    capacity = 5 * token_count * route_count // (4 * experts)
    hidden_units = weight_down.shape[0] * lax.axis_size("dp")
    rows_expert = token_count * route_count * lax.axis_size("dp") // local_experts
    grad_scale = float(rows_expert) ** (-0.5)
    flat_ids = expert_ids.reshape(-1)
    one_hot = (flat_ids[:, None] == jnp.arange(experts, dtype=jnp.int32)[None, :]).astype(jnp.int32)
    ranks = jnp.cumsum(one_hot, axis=0) - 1
    slots = jnp.sum(ranks * one_hot, axis=1)
    target = flat_ids * capacity + slots
    sources = jnp.arange(token_count * route_count, dtype=jnp.int32) // route_count
    inverse = jnp.full((experts * capacity,), token_count, jnp.int32).at[target].set(sources)
    blank = jnp.zeros((1, width), jnp.bfloat16)
    send_tokens = jnp.concatenate([tokens, blank], 0)[inverse].reshape(
        peers, local_experts, capacity, width
    )
    send_grads = jnp.concatenate([cotangent, blank], 0)[inverse].reshape(
        peers, local_experts, capacity, width
    )
    arrived_tokens, arrived_grads = (
        lax.all_to_all(send_tokens, "expert", split_axis=0, concat_axis=0, tiled=True),
        lax.all_to_all(send_grads, "expert", split_axis=0, concat_axis=0, tiled=True),
    )
    full_in, full_down = (
        lax.all_gather(weight_in, "dp", axis=0, tiled=True),
        lax.all_gather(weight_down, "dp", axis=0, tiled=True),
    )
    gate_up = jnp.einsum(
        "secd,dei->seci", arrived_tokens, full_in, preferred_element_type=jnp.float32
    )
    hidden_grad = jnp.einsum(
        "secd,fed->secf", arrived_grads, full_down, preferred_element_type=jnp.float32
    )
    gate = gate_up[..., :hidden_units]
    upper = gate_up[..., hidden_units:]
    sigma = jax.nn.sigmoid(gate)
    grad_gate = hidden_grad * upper * sigma * (1.0 + gate * (1.0 - sigma))
    grad_up = hidden_grad * gate * sigma
    grad_mid = jnp.concatenate([grad_gate, grad_up], -1).astype(jnp.bfloat16)
    input_part = jnp.einsum("seci,dei->secd", grad_mid, full_in, preferred_element_type=jnp.float32)
    input_part = input_part.astype(jnp.bfloat16)
    returned = lax.all_to_all(
        input_part, "expert", split_axis=0, concat_axis=0, tiled=True
    ).reshape(experts * capacity, width)
    picked = returned[target].reshape(token_count, route_count, width)
    token_grad = jnp.sum(route_weights[:, :, None] * picked.astype(jnp.float32), axis=1).astype(
        jnp.bfloat16
    )
    grad_in = lax.psum_scatter(
        (
            jnp.einsum(
                "secd,seci->dei", arrived_tokens, grad_mid, preferred_element_type=jnp.float32
            )
            * grad_scale
        ).astype(jnp.bfloat16),
        "dp",
        scatter_dimension=0,
        tiled=True,
    )
    return (token_grad, grad_in)


LANES = 128
VMEM = 24 * 2**20
NT = (((1,), (1,)), ((), ()))
HIDE = 1 << 34
TN = (((0,), (0,)), ((), ()))


def payload_kernel(tokens, cotangent, ids, weights, out):
    count, width = tokens.shape
    out[:, :width] = tokens[...]
    out[:, width : 2 * width] = cotangent[...]
    lane = lax.broadcasted_iota(jnp.int32, (LANES, count), 0)
    n = LANES // 8
    total = jnp.zeros((LANES, count), jnp.float32)
    routed = jnp.zeros((LANES, count), jnp.float32)
    for k in range(ids.shape[0]):
        here = lane % n == ids[k : k + 1, :]
        total = total + jnp.where(here, weights[k : k + 1, :], 0.0)
        routed = routed + jnp.where(here, 1.0, 0.0)
    top = total.astype(jnp.bfloat16).astype(jnp.float32)
    rest = jnp.where(lane < 2 * n, total - top, jnp.where(lane < 3 * n, routed, 0.0))
    out[:, 2 * width :] = jnp.where(lane < n, top, rest).T.astype(jnp.bfloat16)


def payload_of(tokens, cotangent, ids, weights):
    count, width = tokens.shape
    return pl.pallas_call(
        payload_kernel,
        out_shape=jax.ShapeDtypeStruct((count, 2 * width + LANES), jnp.bfloat16),
        cost_estimate=pl.CostEstimate(flops=1 << 20, bytes_accessed=2 << 20, transcendentals=0),
        name="payload",
    )(tokens, cotangent, ids.T, weights.T)


def halves_kernel(place, weight, kept, given):
    quarter = weight.shape[2] // 4

    def part(k, out):
        for a in range(2):
            both = [weight[e, :, (2 * a + k) * quarter : (2 * a + k + 1) * quarter] for e in range(2)]
            out[:, 2 * a * quarter : 2 * (a + 1) * quarter] = jnp.concatenate(both, 1)

    for high in range(2):

        @pl.when(place[0] // 2 == high)
        def _():
            part(high, kept)
            part(1 - high, given)


def halves(place, weight):
    _, rows, cols = weight.shape
    vmem = pl.BlockSpec(memory_space=pltpu.VMEM)
    return pl.pallas_call(
        halves_kernel,
        in_specs=[pl.BlockSpec(memory_space=pltpu.SMEM), vmem],
        out_specs=[vmem] * 2,
        out_shape=[jax.ShapeDtypeStruct((rows, cols), jnp.bfloat16)] * 2,
        cost_estimate=pl.CostEstimate(flops=HIDE, bytes_accessed=2 << 20, transcendentals=0),
        name="halves",
    )(place, weight)


def join_kernel(place, own, got, far, out):
    quarter = own.shape[1] // 4
    mine = (own[...].astype(jnp.float32) + got[...].astype(jnp.float32)).astype(jnp.bfloat16)

    def put(k, value):
        for a in range(2):
            for e in range(2):
                at = (2 * a + k) * quarter
                out[e, :, at : at + quarter] = value[:, (2 * a + e) * quarter : (2 * a + e + 1) * quarter]

    for high in range(2):

        @pl.when(place[0] // 2 == high)
        def _():
            put(high, mine)
            put(1 - high, far[...])


def join(place, own, got, far):
    vmem = pl.BlockSpec(memory_space=pltpu.VMEM)
    return pl.pallas_call(
        join_kernel,
        in_specs=[pl.BlockSpec(memory_space=pltpu.SMEM)] + [vmem] * 3,
        out_specs=vmem,
        out_shape=jax.ShapeDtypeStruct((2,) + own.shape, jnp.bfloat16),
        cost_estimate=pl.CostEstimate(flops=1 << 20, bytes_accessed=2 << 20, transcendentals=0),
        name="join",
    )(place, own, got, far)


def middle_kernel(place, xs, xo, w0, w1, w2, w3, d0, d1, ts, to, gm_ref, w_all, d_all, pick):
    rows, cols = w0.shape
    ff = d0.shape[0] // 2
    count = xs.shape[0] // 2
    width = ts.shape[1]
    q, j = place[0], place[1]
    hidden = cols // 2
    for k, w in enumerate((w0, w1, w2, w3)):
        w_all[pl.ds(pl.multiple_of((q ^ k) * rows, rows), rows), :] = w[...]
    r = q % 2
    for e in range(2):
        d_all[pl.ds(pl.multiple_of((2 * e + r) * ff, ff), ff), :] = d0[pl.ds(e * ff, ff), :]
        d_all[pl.ds(pl.multiple_of((2 * e + 1 - r) * ff, ff), ff), :] = d1[pl.ds(e * ff, ff), :]
    lane = lax.broadcasted_iota(jnp.int32, (LANES, cols), 0)
    col = lax.broadcasted_iota(jnp.int32, (LANES, cols), 1)
    n = LANES // 8
    expert = 2 * j + jnp.where(col % hidden >= hidden // 2, 1, 0)
    first = jnp.where(col < hidden, expert, expert + 2 * n)
    second = jnp.where(col < hidden, expert + n, -1)
    hit = jnp.where(lane == first, 1.0, 0.0) + jnp.where(lane == second, 1.0, 0.0)
    pick[...] = hit.astype(jnp.bfloat16)

    for b in range(4):
        x_ref, t_ref = (xs, ts) if b < 2 else (xo, to)
        at = pl.ds((b % 2) * count, count)
        gu = jnp.dot(x_ref[at, :width], w_all[...], preferred_element_type=jnp.float32)
        dh = lax.dot_general(
            x_ref[at, width : 2 * width], d_all[...], NT, preferred_element_type=jnp.float32
        )
        wm = jnp.dot(x_ref[at, 2 * width :], pick[...], preferred_element_type=jnp.float32)
        w, on = wm[:, :hidden], wm[:, hidden:]
        gate, up = gu[:, :hidden], gu[:, hidden:]
        sg = 0.5 * jnp.tanh(0.5 * gate) + 0.5
        dhs = dh * on * sg
        gg = dhs * up * (1.0 + gate * (1.0 - sg))
        gup = dhs * gate
        gm_ref[pl.ds(b * count, count), :hidden] = gg.astype(jnp.bfloat16)
        gm_ref[pl.ds(b * count, count), hidden:] = gup.astype(jnp.bfloat16)
        gw = jnp.concatenate([(gg * w).astype(jnp.bfloat16), (gup * w).astype(jnp.bfloat16)], 1)
        t_ref[at, :] = lax.dot_general(
            gw, w_all[...], NT, preferred_element_type=jnp.float32
        ).astype(jnp.bfloat16)


def middle(place, xs, ws, ds):
    n, wide = xs[0].shape
    rows, cols = ws[0].shape
    ffr, width = ds[0].shape
    vmem = pl.BlockSpec(memory_space=pltpu.VMEM)
    return pl.pallas_call(
        middle_kernel,
        in_specs=[pl.BlockSpec(memory_space=pltpu.SMEM)] + [vmem] * 8,
        out_specs=[vmem] * 3,
        scratch_shapes=[
            pltpu.VMEM((4 * rows, cols), jnp.bfloat16),
            pltpu.VMEM((2 * ffr, width), jnp.bfloat16),
            pltpu.VMEM((LANES, cols), jnp.bfloat16),
        ],
        out_shape=[
            jax.ShapeDtypeStruct((n, width), jnp.bfloat16),
            jax.ShapeDtypeStruct((n, width), jnp.bfloat16),
            jax.ShapeDtypeStruct((2 * n, cols), jnp.bfloat16),
        ],
        compiler_params=pltpu.CompilerParams(vmem_limit_bytes=VMEM),
        cost_estimate=pl.CostEstimate(
            flops=HIDE, bytes_accessed=12 << 20, transcendentals=n * cols
        ),
        name="middle",
    )(place, *xs, *ws, *ds)


def outer_kernel(scale, half, count, place, *refs):
    xs, gs, outs = refs[: 2 * half], refs[2 * half : 3 * half], refs[3 * half :]
    acc = None
    for k in range(half):
        x = jnp.concatenate([x[...] for x in xs[2 * k : 2 * k + 2]], 0)
        part = lax.dot_general(x, gs[k][...], TN, preferred_element_type=jnp.float32)
        acc = part if acc is None else acc + part
    value = (acc * scale).astype(jnp.bfloat16)
    for k in range(count):

        @pl.when(pl.program_id(0) == k)
        def _():
            outs[k][...] = value


def outer(place, xs, gs, scale, rows, top, count):
    cols = gs[0].shape[1]
    return pl.pallas_call(
        functools.partial(outer_kernel, scale, len(gs), count),
        grid_spec=pltpu.PrefetchScalarGridSpec(
            num_scalar_prefetch=1,
            grid=(count,),
            in_specs=[pl.BlockSpec((x.shape[0], rows), lambda i, s: (0, s[0] ^ (top - i))) for x in xs]
            + [pl.BlockSpec(g.shape, lambda i, s: (0, 0)) for g in gs],
            out_specs=[pl.BlockSpec((rows, cols), lambda i, s: (0, 0))] * count,
        ),
        out_shape=[jax.ShapeDtypeStruct((rows, cols), jnp.bfloat16)] * count,
        compiler_params=pltpu.CompilerParams(
            vmem_limit_bytes=VMEM, dimension_semantics=("arbitrary",)
        ),
        cost_estimate=pl.CostEstimate(flops=HIDE, bytes_accessed=12 << 20, transcendentals=0),
        name="outer",
    )(place, *xs, *gs)


def by_tokens(tokens, cotangent, expert_ids, route_weights, weight_in, weight_down):
    count, width = tokens.shape
    n_dp = lax.axis_size("dp")
    peers = lax.axis_size("expert")
    half = n_dp // 2
    rows, _, cols = weight_in.shape
    ff_rows = weight_down.shape[0]
    grad_scale = float(count * expert_ids.shape[1] * n_dp // weight_in.shape[1]) ** (-0.5)
    q = lax.axis_index("dp")
    place = jnp.stack([q, lax.axis_index("expert")]).astype(jnp.int32)
    across = [(i, (i + half) % n_dp) for i in range(n_dp)]
    beside = [(i, i ^ 1) for i in range(n_dp)]
    cores = [(i, i ^ 1) for i in range(peers)]
    hops = [[(i, i ^ (2 * m)) for i in range(peers)] for m in (1, 2, 3)]

    payload = payload_of(tokens, cotangent, expert_ids, route_weights)
    far_payload = lax.ppermute(payload, "dp", across)

    def spread(x):
        return [lax.ppermute(x, "expert", hop) for hop in hops]

    def plus(a, b):
        return (a.astype(jnp.float32) + b.astype(jnp.float32)).astype(jnp.bfloat16)

    after = lax.optimization_barrier

    near = [payload] + spread(payload)
    weight_in, weight_down, payload = after((weight_in, weight_down, payload))
    kept, given = halves(place, weight_in.swapaxes(0, 1))
    w1 = lax.ppermute(kept, "dp", beside)
    given, weight_down, w1, far_payload, *near = after((given, weight_down, w1, far_payload, *near))
    near_own = jnp.concatenate(near, 0)
    far = [far_payload] + spread(far_payload)
    w2 = lax.ppermute(given, "dp", across)
    near_sib = lax.ppermute(near_own, "expert", cores)
    near_sib, weight_down = after((near_sib, weight_down))
    down = weight_down.swapaxes(0, 1).reshape(2 * ff_rows, width)
    down1 = lax.ppermute(down, "dp", beside)
    w2, down1, *far = after((w2, down1, *far))
    far_own = jnp.concatenate(far, 0)
    w3 = lax.ppermute(w2, "dp", beside)
    far_sib = lax.ppermute(far_own, "expert", cores)
    ws, ds = (kept, w1, w2, w3), (down, down1)

    def back_sums(own, got):
        return [plus(own[k * count : (k + 1) * count], got[k * count : (k + 1) * count]) for k in range(4)]

    def back_hops(sums):
        return [sums[0]] + [lax.ppermute(t, "expert", hop) for t, hop in zip(sums[1:], hops)]

    near_ts, near_to, near_mid = middle(place, (near_sib, near_own), ws, ds)
    near_got = lax.ppermute(near_ts, "expert", cores)
    far_sib, near_mid = after((far_sib, near_mid))
    far_ts, far_to, far_mid = middle(place, (far_sib, far_own), ws, ds)
    far_got = lax.ppermute(far_ts, "expert", cores)
    tiles, mids = (far_sib, far_own, near_sib, near_own), (far_mid, near_mid)
    (g3,) = outer(place, tiles, mids, grad_scale, rows, 3, 1)
    got3 = lax.ppermute(g3, "dp", beside)
    far_sums, near_sums = back_sums(far_to, far_got), back_sums(near_to, near_got)
    far_mid, *sums = after((far_mid, *far_sums, *near_sums))
    far_sums, near_sums = sums[:4], sums[4:]
    far_back = back_hops(far_sums)
    g2, g1, g0 = outer(place, tiles, (far_mid, near_mid), grad_scale, rows, 2, 3)
    got1 = lax.ppermute(g1, "dp", beside)
    got3, g2, *near_sums = after((got3, g2, *near_sums))
    relay = plus(g2, got3)
    away_half = lax.ppermute(relay, "dp", across)
    near_back = back_hops(near_sums)
    away = sum(t.astype(jnp.float32) for t in far_back).astype(jnp.bfloat16)
    home = lax.ppermute(away, "dp", across)
    near_total = sum(t.astype(jnp.float32) for t in near_back)
    token_grad = (near_total + home.astype(jnp.float32)).astype(jnp.bfloat16)
    grad_in = join(place, g0, got1, away_half).swapaxes(0, 1)
    return token_grad, grad_in


def on_device(tokens, cotangent, expert_ids, route_weights, weight_in, weight_down):
    peers, n_dp = lax.axis_size("expert"), lax.axis_size("dp")
    experts = weight_in.shape[1] * peers
    capacity = 5 * tokens.shape[0] * expert_ids.shape[1] // (4 * experts)
    dense = weight_in.shape[1] * capacity >= tokens.shape[0]
    if dense and weight_in.shape[1] == 2 and n_dp == 4 and peers == 8 and experts == 16:
        form = by_tokens
    else:
        form = by_routes
    return form(tokens, cotangent, expert_ids, route_weights, weight_in, weight_down)


def solution(mesh):
    placed = (
        P(("dp", "expert"), None),
        P(("dp", "expert"), None),
        P(("dp", "expert"), None),
        P(("dp", "expert"), None),
        P("dp", "expert", None),
        P("dp", "expert", None),
    )
    return jax.shard_map(
        on_device,
        mesh=mesh,
        in_specs=placed,
        out_specs=(P(("dp", "expert"), None), P("dp", "expert", None)),
        check_vma=False,
    )
```

```python
import functools

import jax
import jax.numpy as jnp
from jax import lax
from jax.experimental import pallas as pl
from jax.experimental.pallas import tpu as pltpu
from jax.sharding import PartitionSpec as P


def by_routes(tokens, cotangent, expert_ids, route_weights, weight_in, weight_down):
    token_count = tokens.shape[0]
    width = tokens.shape[1]
    route_count = expert_ids.shape[1]
    peers = lax.axis_size("expert")
    local_experts = weight_in.shape[1]
    experts = local_experts * peers
    capacity = 5 * token_count * route_count // (4 * experts)
    hidden_units = weight_down.shape[0] * lax.axis_size("dp")
    rows_expert = token_count * route_count * lax.axis_size("dp") // local_experts
    grad_scale = float(rows_expert) ** (-0.5)
    flat_ids = expert_ids.reshape(-1)
    one_hot = (flat_ids[:, None] == jnp.arange(experts, dtype=jnp.int32)[None, :]).astype(jnp.int32)
    ranks = jnp.cumsum(one_hot, axis=0) - 1
    slots = jnp.sum(ranks * one_hot, axis=1)
    target = flat_ids * capacity + slots
    sources = jnp.arange(token_count * route_count, dtype=jnp.int32) // route_count
    inverse = jnp.full((experts * capacity,), token_count, jnp.int32).at[target].set(sources)
    blank = jnp.zeros((1, width), jnp.bfloat16)
    send_tokens = jnp.concatenate([tokens, blank], 0)[inverse].reshape(
        peers, local_experts, capacity, width
    )
    send_grads = jnp.concatenate([cotangent, blank], 0)[inverse].reshape(
        peers, local_experts, capacity, width
    )
    arrived_tokens, arrived_grads = (
        lax.all_to_all(send_tokens, "expert", split_axis=0, concat_axis=0, tiled=True),
        lax.all_to_all(send_grads, "expert", split_axis=0, concat_axis=0, tiled=True),
    )
    full_in, full_down = (
        lax.all_gather(weight_in, "dp", axis=0, tiled=True),
        lax.all_gather(weight_down, "dp", axis=0, tiled=True),
    )
    gate_up = jnp.einsum(
        "secd,dei->seci", arrived_tokens, full_in, preferred_element_type=jnp.float32
    )
    hidden_grad = jnp.einsum(
        "secd,fed->secf", arrived_grads, full_down, preferred_element_type=jnp.float32
    )
    gate = gate_up[..., :hidden_units]
    upper = gate_up[..., hidden_units:]
    sigma = jax.nn.sigmoid(gate)
    grad_gate = hidden_grad * upper * sigma * (1.0 + gate * (1.0 - sigma))
    grad_up = hidden_grad * gate * sigma
    grad_mid = jnp.concatenate([grad_gate, grad_up], -1).astype(jnp.bfloat16)
    input_part = jnp.einsum("seci,dei->secd", grad_mid, full_in, preferred_element_type=jnp.float32)
    input_part = input_part.astype(jnp.bfloat16)
    returned = lax.all_to_all(
        input_part, "expert", split_axis=0, concat_axis=0, tiled=True
    ).reshape(experts * capacity, width)
    picked = returned[target].reshape(token_count, route_count, width)
    token_grad = jnp.sum(route_weights[:, :, None] * picked.astype(jnp.float32), axis=1).astype(
        jnp.bfloat16
    )
    grad_in = lax.psum_scatter(
        (
            jnp.einsum(
                "secd,seci->dei", arrived_tokens, grad_mid, preferred_element_type=jnp.float32
            )
            * grad_scale
        ).astype(jnp.bfloat16),
        "dp",
        scatter_dimension=0,
        tiled=True,
    )
    return (token_grad, grad_in)


LANES = 128
VMEM = 24 * 2**20
NT = (((1,), (1,)), ((), ()))
HIDE = 1 << 36
SMALL = 8 * 2**20
TN = (((0,), (0,)), ((), ()))


def payload_kernel(tokens, cotangent, ids, weights, out):
    count, width = tokens.shape
    out[:, :width] = tokens[...]
    out[:, width : 2 * width] = cotangent[...]
    lane = lax.broadcasted_iota(jnp.int32, (LANES, count), 0)
    n = LANES // 8
    total = jnp.zeros((LANES, count), jnp.float32)
    routed = jnp.zeros((LANES, count), jnp.float32)
    for k in range(ids.shape[0]):
        here = lane % n == ids[k : k + 1, :]
        total = total + jnp.where(here, weights[k : k + 1, :], 0.0)
        routed = routed + jnp.where(here, 1.0, 0.0)
    top = total.astype(jnp.bfloat16).astype(jnp.float32)
    rest = jnp.where(lane < 2 * n, total - top, jnp.where(lane < 3 * n, routed, 0.0))
    out[:, 2 * width :] = jnp.where(lane < n, top, rest).T.astype(jnp.bfloat16)


def payload_of(tokens, cotangent, ids, weights):
    count, width = tokens.shape
    return pl.pallas_call(
        payload_kernel,
        out_shape=jax.ShapeDtypeStruct((count, 2 * width + LANES), jnp.bfloat16),
        cost_estimate=pl.CostEstimate(flops=1 << 20, bytes_accessed=2 << 20, transcendentals=0),
        name="payload",
    )(tokens, cotangent, ids.T, weights.T)


def halves_kernel(place, weight, kept, given):
    quarter = weight.shape[2] // 4

    def part(k, out):
        for a in range(2):
            both = [weight[e, :, (2 * a + k) * quarter : (2 * a + k + 1) * quarter] for e in range(2)]
            out[:, 2 * a * quarter : 2 * (a + 1) * quarter] = jnp.concatenate(both, 1)

    for high in range(2):

        @pl.when(place[0] // 2 == high)
        def _():
            part(high, kept)
            part(1 - high, given)


def halves(place, weight):
    _, rows, cols = weight.shape
    vmem = pl.BlockSpec(memory_space=pltpu.VMEM)
    return pl.pallas_call(
        halves_kernel,
        in_specs=[pl.BlockSpec(memory_space=pltpu.SMEM), vmem],
        out_specs=[vmem] * 2,
        out_shape=[jax.ShapeDtypeStruct((rows, cols), jnp.bfloat16)] * 2,
        cost_estimate=pl.CostEstimate(flops=HIDE, bytes_accessed=2 << 20, transcendentals=0),
        compiler_params=pltpu.CompilerParams(vmem_limit_bytes=SMALL),
        name="halves",
    )(place, weight)


def join_kernel(place, own, got, far, out):
    quarter = own.shape[1] // 4
    mine = (own[...].astype(jnp.float32) + got[...].astype(jnp.float32)).astype(jnp.bfloat16)

    def put(k, value):
        for a in range(2):
            for e in range(2):
                at = (2 * a + k) * quarter
                out[e, :, at : at + quarter] = value[:, (2 * a + e) * quarter : (2 * a + e + 1) * quarter]

    for high in range(2):

        @pl.when(place[0] // 2 == high)
        def _():
            put(high, mine)
            put(1 - high, far[...])


def join(place, own, got, far):
    vmem = pl.BlockSpec(memory_space=pltpu.VMEM)
    return pl.pallas_call(
        join_kernel,
        in_specs=[pl.BlockSpec(memory_space=pltpu.SMEM)] + [vmem] * 3,
        out_specs=vmem,
        out_shape=jax.ShapeDtypeStruct((2,) + own.shape, jnp.bfloat16),
        cost_estimate=pl.CostEstimate(flops=1 << 20, bytes_accessed=2 << 20, transcendentals=0),
        compiler_params=pltpu.CompilerParams(vmem_limit_bytes=SMALL),
        name="join",
    )(place, own, got, far)


def gather_weights(place, ws, ds, w_all, d_all, pick):
    rows, cols = ws[0].shape
    ff = ds[0].shape[0] // 2
    q, j = place[0], place[1]
    hidden = cols // 2
    for k, w in enumerate(ws):
        w_all[pl.ds(pl.multiple_of((q ^ k) * rows, rows), rows), :] = w[...]
    r = q % 2
    for e in range(2):
        d_all[pl.ds(pl.multiple_of((2 * e + r) * ff, ff), ff), :] = ds[0][pl.ds(e * ff, ff), :]
        d_all[pl.ds(pl.multiple_of((2 * e + 1 - r) * ff, ff), ff), :] = ds[1][pl.ds(e * ff, ff), :]
    lane = lax.broadcasted_iota(jnp.int32, (LANES, cols), 0)
    col = lax.broadcasted_iota(jnp.int32, (LANES, cols), 1)
    n = LANES // 8
    expert = 2 * j + jnp.where(col % hidden >= hidden // 2, 1, 0)
    first = jnp.where(col < hidden, expert, expert + 2 * n)
    second = jnp.where(col < hidden, expert + n, -1)
    hit = jnp.where(lane == first, 1.0, 0.0) + jnp.where(lane == second, 1.0, 0.0)
    pick[...] = hit.astype(jnp.bfloat16)


def grad_mid(xs, xo, w_all, d_all, pick, gm, gw):
    width, cols = w_all.shape
    hidden = cols // 2
    count = xs.shape[0] // 2
    for b in range(4):
        x = xs if b < 2 else xo
        at, to = pl.ds((b % 2) * count, count), pl.ds(b * count, count)
        gu = jnp.dot(x[at, :width], w_all[...], preferred_element_type=jnp.float32)
        dh = lax.dot_general(
            x[at, width : 2 * width], d_all[...], NT, preferred_element_type=jnp.float32
        )
        wm = jnp.dot(x[at, 2 * width :], pick[...], preferred_element_type=jnp.float32)
        w, on = wm[:, :hidden], wm[:, hidden:]
        gate, up = gu[:, :hidden], gu[:, hidden:]
        sg = 0.5 * jnp.tanh(0.5 * gate) + 0.5
        dhs = dh * on * sg
        gg = dhs * up * (1.0 + gate * (1.0 - sg))
        gup = dhs * gate
        gm[to, :hidden] = gg.astype(jnp.bfloat16)
        gm[to, hidden:] = gup.astype(jnp.bfloat16)
        gw[to, :hidden] = (gg * w).astype(jnp.bfloat16)
        gw[to, hidden:] = (gup * w).astype(jnp.bfloat16)


def weights_kernel(place, w0, w1, w2, w3, d0, d1, w_all, d_all, pick):
    gather_weights(place, (w0, w1, w2, w3), (d0, d1), w_all, d_all, pick)


def vmem_call(kernel, name, outs, *args, place=None, flops=HIDE):
    vmem = pl.BlockSpec(memory_space=pltpu.VMEM)
    specs = [vmem] * len(args)
    if place is not None:
        args, specs = (place, *args), [pl.BlockSpec(memory_space=pltpu.SMEM)] + specs
    return pl.pallas_call(
        kernel,
        in_specs=specs,
        out_specs=[vmem] * len(outs),
        out_shape=[jax.ShapeDtypeStruct(o, jnp.bfloat16) for o in outs],
        compiler_params=pltpu.CompilerParams(vmem_limit_bytes=VMEM),
        cost_estimate=pl.CostEstimate(flops=flops, bytes_accessed=12 << 20, transcendentals=0),
        name=name,
    )(*args)


def token_kernel(gw, w_all, ts, to):
    n = ts.shape[0]
    for b, out in enumerate((ts, to)):
        out[...] = lax.dot_general(
            gw[pl.ds(b * n, n), :], w_all[...], NT, preferred_element_type=jnp.float32
        ).astype(jnp.bfloat16)


def outer_kernel(scale, half, count, place, *refs):
    xs, gs, outs = refs[: 2 * half], refs[2 * half : 3 * half], refs[3 * half :]
    acc = None
    for k in range(half):
        x = jnp.concatenate([x[...] for x in xs[2 * k : 2 * k + 2]], 0)
        part = lax.dot_general(x, gs[k][...], TN, preferred_element_type=jnp.float32)
        acc = part if acc is None else acc + part
    value = (acc * scale).astype(jnp.bfloat16)
    for k in range(count):

        @pl.when(pl.program_id(0) == k)
        def _():
            outs[k][...] = value


def outer(place, xs, gs, scale, rows, top, count):
    cols = gs[0].shape[1]
    return pl.pallas_call(
        functools.partial(outer_kernel, scale, len(gs), count),
        grid_spec=pltpu.PrefetchScalarGridSpec(
            num_scalar_prefetch=1,
            grid=(count,),
            in_specs=[pl.BlockSpec((x.shape[0], rows), lambda i, s: (0, s[0] ^ (top - i))) for x in xs]
            + [pl.BlockSpec(g.shape, lambda i, s: (0, 0)) for g in gs],
            out_specs=[pl.BlockSpec((rows, cols), lambda i, s: (0, 0))] * count,
        ),
        out_shape=[jax.ShapeDtypeStruct((rows, cols), jnp.bfloat16)] * count,
        compiler_params=pltpu.CompilerParams(
            vmem_limit_bytes=VMEM, dimension_semantics=("arbitrary",)
        ),
        cost_estimate=pl.CostEstimate(flops=HIDE, bytes_accessed=12 << 20, transcendentals=0),
        name="outer",
    )(place, *xs, *gs)


def by_tokens(tokens, cotangent, expert_ids, route_weights, weight_in, weight_down):
    count, width = tokens.shape
    n_dp = lax.axis_size("dp")
    peers = lax.axis_size("expert")
    half = n_dp // 2
    rows, _, cols = weight_in.shape
    ff_rows = weight_down.shape[0]
    grad_scale = float(count * expert_ids.shape[1] * n_dp // weight_in.shape[1]) ** (-0.5)
    q = lax.axis_index("dp")
    place = jnp.stack([q, lax.axis_index("expert")]).astype(jnp.int32)
    across = [(i, (i + half) % n_dp) for i in range(n_dp)]
    beside = [(i, i ^ 1) for i in range(n_dp)]
    cores = [(i, i ^ 1) for i in range(peers)]
    hops = [[(i, i ^ (2 * m)) for i in range(peers)] for m in (1, 2, 3)]

    payload = payload_of(tokens, cotangent, expert_ids, route_weights)

    def spread(x):
        return [lax.ppermute(x, "expert", hop) for hop in hops]

    def plus(a, b):
        return (a.astype(jnp.float32) + b.astype(jnp.float32)).astype(jnp.bfloat16)

    after = lax.optimization_barrier

    near = [payload] + spread(payload)
    far_payload = lax.ppermute(payload, "dp", across)
    down1 = lax.ppermute(weight_down, "dp", beside)
    weight_in, payload = after((weight_in, payload))
    kept, given = halves(place, weight_in.swapaxes(0, 1))
    given, kept, far_payload, down1, *near = after((given, kept, far_payload, down1, *near))
    far = [far_payload] + spread(far_payload)
    w2 = lax.ppermute(given, "dp", across)
    w1 = lax.ppermute(kept, "dp", beside)
    downs = [d.swapaxes(0, 1).reshape(2 * ff_rows, width) for d in (weight_down, down1)]
    w2, w1, far[0] = after((w2, w1, far[0]))
    w3 = lax.ppermute(w2, "dp", beside)
    far_own = jnp.concatenate(far, 0)
    far_sib = lax.ppermute(far_own, "expert", cores)
    near_own = jnp.concatenate(near, 0)
    tall, wide = near_own.shape
    cols = kept.shape[1]
    mid_shape, token_shape = (2 * tall, cols), (tall, width)
    w_all, d_all, pick = vmem_call(
        weights_kernel,
        "weights",
        [(width, cols), (4 * ff_rows, width), (LANES, cols)],
        *(kept, w1, w2, w3, *downs),
        place=place,
    )
    far_sib, w_all, near_own = after((far_sib, w_all, near_own))
    near_sib = lax.ppermute(near_own, "expert", cores)

    def back_sums(own, got):
        return [plus(own[k * count : (k + 1) * count], got[k * count : (k + 1) * count]) for k in range(4)]

    def back_hops(sums):
        return [sums[0]] + [lax.ppermute(t, "expert", hop) for t, hop in zip(sums[1:], hops)]

    def mids(name, sib, own):
        return vmem_call(grad_mid, name, [mid_shape, mid_shape], sib, own, w_all, d_all, pick)

    def backs(name, gw):
        return vmem_call(
            token_kernel, name, [token_shape] * 2, gw, w_all, flops=4 * tall * cols * width
        )

    far_mid, far_gw = mids("far", far_sib, far_own)
    far_ts, far_to = backs("far_tokens", far_gw)
    far_got = lax.ppermute(far_ts, "expert", cores)
    near_sib, far_to = after((near_sib, far_to))
    near_mid, near_gw = mids("near", near_sib, near_own)
    far_got, near_mid = after((far_got, near_mid))
    far_sums = back_sums(far_to, far_got)
    near_mid, *far_sums = after((near_mid, *far_sums))
    far_back = back_hops(far_sums)
    tiles = (far_sib, far_own, near_sib, near_own)
    (g3,) = outer(place, tiles, (far_mid, near_mid), grad_scale, rows, 3, 1)
    got3 = lax.ppermute(g3, "dp", beside)
    near_gw, g3 = after((near_gw, g3))
    near_ts, near_to = backs("near_tokens", near_gw)
    near_got = lax.ppermute(near_ts, "expert", cores)
    near_mid, near_to = after((near_mid, near_to))
    g2, g1 = outer(place, tiles, (far_mid, near_mid), grad_scale, rows, 2, 2)
    near_got, g1 = after((near_got, g1))
    got1 = lax.ppermute(g1, "dp", beside)
    near_sums = back_sums(near_to, near_got)
    near_mid, g1 = after((near_mid, g1))
    (g0,) = outer(place, tiles, (far_mid, near_mid), grad_scale, rows, 0, 1)
    got3, g0, *far_back = after((got3, g0, *far_back))
    relay = plus(g2, got3)
    away_half = lax.ppermute(relay, "dp", across)
    away = sum(t.astype(jnp.float32) for t in far_back).astype(jnp.bfloat16)
    home = lax.ppermute(away, "dp", across)
    *near_sums, got1 = after((*near_sums, got1))
    near_back = back_hops(near_sums)
    near_total = sum(t.astype(jnp.float32) for t in near_back)
    token_grad = (near_total + home.astype(jnp.float32)).astype(jnp.bfloat16)
    grad_in = join(place, g0, got1, away_half).swapaxes(0, 1)
    return token_grad, grad_in


def on_device(tokens, cotangent, expert_ids, route_weights, weight_in, weight_down):
    peers, n_dp = lax.axis_size("expert"), lax.axis_size("dp")
    experts = weight_in.shape[1] * peers
    capacity = 5 * tokens.shape[0] * expert_ids.shape[1] // (4 * experts)
    dense = weight_in.shape[1] * capacity >= tokens.shape[0]
    if dense and weight_in.shape[1] == 2 and n_dp == 4 and peers == 8 and experts == 16:
        form = by_tokens
    else:
        form = by_routes
    return form(tokens, cotangent, expert_ids, route_weights, weight_in, weight_down)


def solution(mesh):
    placed = (
        P(("dp", "expert"), None),
        P(("dp", "expert"), None),
        P(("dp", "expert"), None),
        P(("dp", "expert"), None),
        P("dp", "expert", None),
        P("dp", "expert", None),
    )
    return jax.shard_map(
        on_device,
        mesh=mesh,
        in_specs=placed,
        out_specs=(P(("dp", "expert"), None), P("dp", "expert", None)),
        check_vma=False,
    )
```

```python
import functools

import jax
import jax.numpy as jnp
from jax import lax
from jax.experimental import pallas as pl
from jax.experimental.pallas import tpu as pltpu
from jax.sharding import PartitionSpec as P


def by_routes(tokens, cotangent, expert_ids, route_weights, weight_in, weight_down):
    token_count = tokens.shape[0]
    width = tokens.shape[1]
    route_count = expert_ids.shape[1]
    peers = lax.axis_size("expert")
    local_experts = weight_in.shape[1]
    experts = local_experts * peers
    capacity = 5 * token_count * route_count // (4 * experts)
    hidden_units = weight_down.shape[0] * lax.axis_size("dp")
    rows_expert = token_count * route_count * lax.axis_size("dp") // local_experts
    grad_scale = float(rows_expert) ** (-0.5)
    flat_ids = expert_ids.reshape(-1)
    one_hot = (flat_ids[:, None] == jnp.arange(experts, dtype=jnp.int32)[None, :]).astype(jnp.int32)
    ranks = jnp.cumsum(one_hot, axis=0) - 1
    slots = jnp.sum(ranks * one_hot, axis=1)
    target = flat_ids * capacity + slots
    sources = jnp.arange(token_count * route_count, dtype=jnp.int32) // route_count
    inverse = jnp.full((experts * capacity,), token_count, jnp.int32).at[target].set(sources)
    blank = jnp.zeros((1, width), jnp.bfloat16)
    send_tokens = jnp.concatenate([tokens, blank], 0)[inverse].reshape(
        peers, local_experts, capacity, width
    )
    send_grads = jnp.concatenate([cotangent, blank], 0)[inverse].reshape(
        peers, local_experts, capacity, width
    )
    arrived_tokens, arrived_grads = (
        lax.all_to_all(send_tokens, "expert", split_axis=0, concat_axis=0, tiled=True),
        lax.all_to_all(send_grads, "expert", split_axis=0, concat_axis=0, tiled=True),
    )
    full_in, full_down = (
        lax.all_gather(weight_in, "dp", axis=0, tiled=True),
        lax.all_gather(weight_down, "dp", axis=0, tiled=True),
    )
    gate_up = jnp.einsum(
        "secd,dei->seci", arrived_tokens, full_in, preferred_element_type=jnp.float32
    )
    hidden_grad = jnp.einsum(
        "secd,fed->secf", arrived_grads, full_down, preferred_element_type=jnp.float32
    )
    gate = gate_up[..., :hidden_units]
    upper = gate_up[..., hidden_units:]
    sigma = jax.nn.sigmoid(gate)
    grad_gate = hidden_grad * upper * sigma * (1.0 + gate * (1.0 - sigma))
    grad_up = hidden_grad * gate * sigma
    grad_mid = jnp.concatenate([grad_gate, grad_up], -1).astype(jnp.bfloat16)
    input_part = jnp.einsum("seci,dei->secd", grad_mid, full_in, preferred_element_type=jnp.float32)
    input_part = input_part.astype(jnp.bfloat16)
    returned = lax.all_to_all(
        input_part, "expert", split_axis=0, concat_axis=0, tiled=True
    ).reshape(experts * capacity, width)
    picked = returned[target].reshape(token_count, route_count, width)
    token_grad = jnp.sum(route_weights[:, :, None] * picked.astype(jnp.float32), axis=1).astype(
        jnp.bfloat16
    )
    grad_in = lax.psum_scatter(
        (
            jnp.einsum(
                "secd,seci->dei", arrived_tokens, grad_mid, preferred_element_type=jnp.float32
            )
            * grad_scale
        ).astype(jnp.bfloat16),
        "dp",
        scatter_dimension=0,
        tiled=True,
    )
    return (token_grad, grad_in)


LANES = 128
VMEM = 24 * 2**20
NT = (((1,), (1,)), ((), ()))
HIDE = 1 << 36
SMALL = 8 * 2**20
TN = (((0,), (0,)), ((), ()))


def payload_kernel(tokens, cotangent, ids, weights, out):
    count, width = tokens.shape
    out[:, :width] = tokens[...]
    out[:, width : 2 * width] = cotangent[...]
    lane = lax.broadcasted_iota(jnp.int32, (LANES, count), 0)
    n = LANES // 8
    total = jnp.zeros((LANES, count), jnp.float32)
    routed = jnp.zeros((LANES, count), jnp.float32)
    for k in range(ids.shape[0]):
        here = lane % n == ids[k : k + 1, :]
        total = total + jnp.where(here, weights[k : k + 1, :], 0.0)
        routed = routed + jnp.where(here, 1.0, 0.0)
    top = total.astype(jnp.bfloat16).astype(jnp.float32)
    rest = jnp.where(lane < 2 * n, total - top, jnp.where(lane < 3 * n, routed, 0.0))
    out[:, 2 * width :] = jnp.where(lane < n, top, rest).T.astype(jnp.bfloat16)


def payload_of(tokens, cotangent, ids, weights):
    count, width = tokens.shape
    return pl.pallas_call(
        payload_kernel,
        out_shape=jax.ShapeDtypeStruct((count, 2 * width + LANES), jnp.bfloat16),
        cost_estimate=pl.CostEstimate(flops=1 << 20, bytes_accessed=2 << 20, transcendentals=0),
        name="payload",
    )(tokens, cotangent, ids.T, weights.T)


def halves_kernel(place, weight, kept, given):
    quarter = weight.shape[2] // 4

    def part(k, out):
        for a in range(2):
            both = [weight[e, :, (2 * a + k) * quarter : (2 * a + k + 1) * quarter] for e in range(2)]
            out[:, 2 * a * quarter : 2 * (a + 1) * quarter] = jnp.concatenate(both, 1)

    for high in range(2):

        @pl.when(place[0] // 2 == high)
        def _():
            part(high, kept)
            part(1 - high, given)


def halves(place, weight):
    _, rows, cols = weight.shape
    vmem = pl.BlockSpec(memory_space=pltpu.VMEM)
    return pl.pallas_call(
        halves_kernel,
        in_specs=[pl.BlockSpec(memory_space=pltpu.SMEM), vmem],
        out_specs=[vmem] * 2,
        out_shape=[jax.ShapeDtypeStruct((rows, cols), jnp.bfloat16)] * 2,
        cost_estimate=pl.CostEstimate(flops=1 << 20, bytes_accessed=2 << 20, transcendentals=0),
        compiler_params=pltpu.CompilerParams(vmem_limit_bytes=SMALL),
        name="halves",
    )(place, weight)


def join_kernel(place, own, got, far, out):
    quarter = own.shape[1] // 4
    mine = (own[...].astype(jnp.float32) + got[...].astype(jnp.float32)).astype(jnp.bfloat16)

    def put(k, value):
        for a in range(2):
            for e in range(2):
                at = (2 * a + k) * quarter
                out[e, :, at : at + quarter] = value[:, (2 * a + e) * quarter : (2 * a + e + 1) * quarter]

    for high in range(2):

        @pl.when(place[0] // 2 == high)
        def _():
            put(high, mine)
            put(1 - high, far[...])


def join(place, own, got, far):
    vmem = pl.BlockSpec(memory_space=pltpu.VMEM)
    return pl.pallas_call(
        join_kernel,
        in_specs=[pl.BlockSpec(memory_space=pltpu.SMEM)] + [vmem] * 3,
        out_specs=vmem,
        out_shape=jax.ShapeDtypeStruct((2,) + own.shape, jnp.bfloat16),
        cost_estimate=pl.CostEstimate(flops=1 << 20, bytes_accessed=2 << 20, transcendentals=0),
        compiler_params=pltpu.CompilerParams(vmem_limit_bytes=SMALL),
        name="join",
    )(place, own, got, far)


def gather_weights(place, ws, ds, w_all, d_all, pick):
    rows, cols = ws[0].shape
    ff = ds[0].shape[0] // 2
    q, j = place[0], place[1]
    hidden = cols // 2
    for k, w in enumerate(ws):
        w_all[pl.ds(pl.multiple_of((q ^ k) * rows, rows), rows), :] = w[...]
    r = q % 2
    for e in range(2):
        d_all[pl.ds(pl.multiple_of((2 * e + r) * ff, ff), ff), :] = ds[0][pl.ds(e * ff, ff), :]
        d_all[pl.ds(pl.multiple_of((2 * e + 1 - r) * ff, ff), ff), :] = ds[1][pl.ds(e * ff, ff), :]
    lane = lax.broadcasted_iota(jnp.int32, (LANES, cols), 0)
    col = lax.broadcasted_iota(jnp.int32, (LANES, cols), 1)
    n = LANES // 8
    expert = 2 * j + jnp.where(col % hidden >= hidden // 2, 1, 0)
    first = jnp.where(col < hidden, expert, expert + 2 * n)
    second = jnp.where(col < hidden, expert + n, -1)
    hit = jnp.where(lane == first, 1.0, 0.0) + jnp.where(lane == second, 1.0, 0.0)
    pick[...] = hit.astype(jnp.bfloat16)


def grad_mid(xs, xo, w_all, d_all, pick, gm, gw):
    width, cols = w_all.shape
    hidden = cols // 2
    count = xs.shape[0] // 2
    for b in range(4):
        x = xs if b < 2 else xo
        at, to = pl.ds((b % 2) * count, count), pl.ds(b * count, count)
        gu = jnp.dot(x[at, :width], w_all[...], preferred_element_type=jnp.float32)
        dh = lax.dot_general(
            x[at, width : 2 * width], d_all[...], NT, preferred_element_type=jnp.float32
        )
        wm = jnp.dot(x[at, 2 * width :], pick[...], preferred_element_type=jnp.float32)
        w, on = wm[:, :hidden], wm[:, hidden:]
        gate, up = gu[:, :hidden], gu[:, hidden:]
        sg = 0.5 * jnp.tanh(0.5 * gate) + 0.5
        dhs = dh * on * sg
        gg = dhs * up * (1.0 + gate * (1.0 - sg))
        gup = dhs * gate
        gm[to, :hidden] = gg.astype(jnp.bfloat16)
        gm[to, hidden:] = gup.astype(jnp.bfloat16)
        gw[to, :hidden] = (gg * w).astype(jnp.bfloat16)
        gw[to, hidden:] = (gup * w).astype(jnp.bfloat16)


def weights_kernel(place, w0, w1, w2, w3, d0, d1, w_all, d_all, pick):
    gather_weights(place, (w0, w1, w2, w3), (d0, d1), w_all, d_all, pick)


def vmem_call(kernel, name, outs, *args, place=None, flops=HIDE):
    vmem = pl.BlockSpec(memory_space=pltpu.VMEM)
    specs = [vmem] * len(args)
    if place is not None:
        args, specs = (place, *args), [pl.BlockSpec(memory_space=pltpu.SMEM)] + specs
    return pl.pallas_call(
        kernel,
        in_specs=specs,
        out_specs=[vmem] * len(outs),
        out_shape=[jax.ShapeDtypeStruct(o, jnp.bfloat16) for o in outs],
        compiler_params=pltpu.CompilerParams(vmem_limit_bytes=VMEM),
        cost_estimate=pl.CostEstimate(flops=flops, bytes_accessed=12 << 20, transcendentals=0),
        name=name,
    )(*args)


def token_kernel(gw, w_all, ts, to):
    n = ts.shape[0]
    for b, out in enumerate((ts, to)):
        out[...] = lax.dot_general(
            gw[pl.ds(b * n, n), :], w_all[...], NT, preferred_element_type=jnp.float32
        ).astype(jnp.bfloat16)


def outer_kernel(scale, half, count, place, *refs):
    xs, gs, outs = refs[: 2 * half], refs[2 * half : 3 * half], refs[3 * half :]
    acc = None
    for k in range(half):
        x = jnp.concatenate([x[...] for x in xs[2 * k : 2 * k + 2]], 0)
        part = lax.dot_general(x, gs[k][...], TN, preferred_element_type=jnp.float32)
        acc = part if acc is None else acc + part
    value = (acc * scale).astype(jnp.bfloat16)
    for k in range(count):

        @pl.when(pl.program_id(0) == k)
        def _():
            outs[k][...] = value


def outer(place, xs, gs, scale, rows, top, count, flops=HIDE):
    cols = gs[0].shape[1]
    return pl.pallas_call(
        functools.partial(outer_kernel, scale, len(gs), count),
        grid_spec=pltpu.PrefetchScalarGridSpec(
            num_scalar_prefetch=1,
            grid=(count,),
            in_specs=[pl.BlockSpec((x.shape[0], rows), lambda i, s: (0, s[0] ^ (top - i))) for x in xs]
            + [pl.BlockSpec(g.shape, lambda i, s: (0, 0)) for g in gs],
            out_specs=[pl.BlockSpec((rows, cols), lambda i, s: (0, 0))] * count,
        ),
        out_shape=[jax.ShapeDtypeStruct((rows, cols), jnp.bfloat16)] * count,
        compiler_params=pltpu.CompilerParams(
            vmem_limit_bytes=VMEM, dimension_semantics=("arbitrary",)
        ),
        cost_estimate=pl.CostEstimate(flops=flops, bytes_accessed=12 << 20, transcendentals=0),
        name="outer",
    )(place, *xs, *gs)


def by_tokens(tokens, cotangent, expert_ids, route_weights, weight_in, weight_down):
    count, width = tokens.shape
    n_dp = lax.axis_size("dp")
    peers = lax.axis_size("expert")
    half = n_dp // 2
    rows, _, cols = weight_in.shape
    ff_rows = weight_down.shape[0]
    grad_scale = float(count * expert_ids.shape[1] * n_dp // weight_in.shape[1]) ** (-0.5)
    q = lax.axis_index("dp")
    place = jnp.stack([q, lax.axis_index("expert")]).astype(jnp.int32)
    across = [(i, (i + half) % n_dp) for i in range(n_dp)]
    beside = [(i, i ^ 1) for i in range(n_dp)]
    cores = [(i, i ^ 1) for i in range(peers)]
    hops = [[(i, i ^ (2 * m)) for i in range(peers)] for m in (1, 2, 3)]

    payload = payload_of(tokens, cotangent, expert_ids, route_weights)

    def spread(x):
        return [lax.ppermute(x, "expert", hop) for hop in hops]

    def plus(a, b):
        return (a.astype(jnp.float32) + b.astype(jnp.float32)).astype(jnp.bfloat16)

    after = lax.optimization_barrier

    near = [payload] + spread(payload)
    far_payload = lax.ppermute(payload, "dp", across)
    down1 = lax.ppermute(weight_down, "dp", beside)
    weight_in, payload = after((weight_in, payload))
    kept, given = halves(place, weight_in.swapaxes(0, 1))
    given, kept, far_payload = after((given, kept, far_payload))
    far = [far_payload] + spread(far_payload)
    w2 = lax.ppermute(given, "dp", across)
    w1 = lax.ppermute(kept, "dp", beside)
    downs = [d.swapaxes(0, 1).reshape(2 * ff_rows, width) for d in (weight_down, down1)]
    w2, w1, far[0] = after((w2, w1, far[0]))
    w3 = lax.ppermute(w2, "dp", beside)
    far_own = jnp.concatenate(far, 0)
    far_sib = lax.ppermute(far_own, "expert", cores)
    near_own = jnp.concatenate(near, 0)
    tall, wide = near_own.shape
    cols = kept.shape[1]
    mid_shape, token_shape = (2 * tall, cols), (tall, width)
    w_all, d_all, pick = vmem_call(
        weights_kernel,
        "weights",
        [(width, cols), (4 * ff_rows, width), (LANES, cols)],
        *(kept, w1, w2, w3, *downs),
        place=place,
    )
    far_sib, w_all, near_own = after((far_sib, w_all, near_own))
    near_sib = lax.ppermute(near_own, "expert", cores)

    def back_sums(own, got):
        return [plus(own[k * count : (k + 1) * count], got[k * count : (k + 1) * count]) for k in range(4)]

    def back_hops(sums):
        return [sums[0]] + [lax.ppermute(t, "expert", hop) for t, hop in zip(sums[1:], hops)]

    def mids(name, sib, own):
        return vmem_call(grad_mid, name, [mid_shape, mid_shape], sib, own, w_all, d_all, pick)

    def backs(name, gw):
        return vmem_call(
            token_kernel, name, [token_shape] * 2, gw, w_all, flops=4 * tall * cols * width
        )

    far_mid, far_gw = mids("far", far_sib, far_own)
    near_sib, far_mid = after((near_sib, far_mid))
    near_mid, near_gw = mids("near", near_sib, near_own)
    tiles = (far_sib, far_own, near_sib, near_own)
    (g3,) = outer(place, tiles, (far_mid, near_mid), grad_scale, rows, 3, 1)
    got3 = lax.ppermute(g3, "dp", beside)
    near_gw, g3 = after((near_gw, g3))
    near_ts, near_to = backs("near_tokens", near_gw)
    near_got = lax.ppermute(near_ts, "expert", cores)
    far_gw, near_to = after((far_gw, near_to))
    far_ts, far_to = backs("far_tokens", far_gw)
    far_got = lax.ppermute(far_ts, "expert", cores)
    near_mid, far_to = after((near_mid, far_to))
    g2, g1 = outer(place, tiles, (far_mid, near_mid), grad_scale, rows, 2, 2)
    got1 = lax.ppermute(g1, "dp", beside)
    far_got, near_got, g2 = after((far_got, near_got, g2))
    far_sums, near_sums = back_sums(far_to, far_got), back_sums(near_to, near_got)
    got3, *near_sums = after((got3, *near_sums))
    relay = plus(g2, got3)
    away_half = lax.ppermute(relay, "dp", across)
    near_mid, relay = after((near_mid, relay))
    (g0,) = outer(place, tiles, (far_mid, near_mid), grad_scale, rows, 0, 1, HIDE)
    g0, *far_sums = after((g0, *far_sums))
    far_back = back_hops(far_sums)
    away_half, got1, *far_back = after((away_half, got1, *far_back))
    away = sum(t.astype(jnp.float32) for t in far_back).astype(jnp.bfloat16)
    away, *near_sums = after((away, *near_sums))
    home = lax.ppermute(away, "dp", across)
    near_back = back_hops(near_sums)
    grad_in = join(place, g0, got1, away_half).swapaxes(0, 1)
    total = near_back[0].astype(jnp.float32) + home.astype(jnp.float32)
    total, *near_back = after((total, *near_back[1:]))
    token_grad = sum((t.astype(jnp.float32) for t in near_back), total).astype(jnp.bfloat16)
    return token_grad, grad_in


def on_device(tokens, cotangent, expert_ids, route_weights, weight_in, weight_down):
    peers, n_dp = lax.axis_size("expert"), lax.axis_size("dp")
    experts = weight_in.shape[1] * peers
    capacity = 5 * tokens.shape[0] * expert_ids.shape[1] // (4 * experts)
    dense = weight_in.shape[1] * capacity >= tokens.shape[0]
    if dense and weight_in.shape[1] == 2 and n_dp == 4 and peers == 8 and experts == 16:
        form = by_tokens
    else:
        form = by_routes
    return form(tokens, cotangent, expert_ids, route_weights, weight_in, weight_down)


def solution(mesh):
    placed = (
        P(("dp", "expert"), None),
        P(("dp", "expert"), None),
        P(("dp", "expert"), None),
        P(("dp", "expert"), None),
        P("dp", "expert", None),
        P("dp", "expert", None),
    )
    return jax.shard_map(
        on_device,
        mesh=mesh,
        in_specs=placed,
        out_specs=(P(("dp", "expert"), None), P("dp", "expert", None)),
        check_vma=False,
    )
```

```python
import functools

import jax
import jax.numpy as jnp
from jax import lax
from jax.experimental import pallas as pl
from jax.experimental.pallas import tpu as pltpu
from jax.sharding import PartitionSpec as P


def by_routes(tokens, cotangent, expert_ids, route_weights, weight_in, weight_down):
    token_count = tokens.shape[0]
    width = tokens.shape[1]
    route_count = expert_ids.shape[1]
    peers = lax.axis_size("expert")
    local_experts = weight_in.shape[1]
    experts = local_experts * peers
    capacity = 5 * token_count * route_count // (4 * experts)
    hidden_units = weight_down.shape[0] * lax.axis_size("dp")
    rows_expert = token_count * route_count * lax.axis_size("dp") // local_experts
    grad_scale = float(rows_expert) ** (-0.5)
    flat_ids = expert_ids.reshape(-1)
    one_hot = (flat_ids[:, None] == jnp.arange(experts, dtype=jnp.int32)[None, :]).astype(jnp.int32)
    ranks = jnp.cumsum(one_hot, axis=0) - 1
    slots = jnp.sum(ranks * one_hot, axis=1)
    target = flat_ids * capacity + slots
    sources = jnp.arange(token_count * route_count, dtype=jnp.int32) // route_count
    inverse = jnp.full((experts * capacity,), token_count, jnp.int32).at[target].set(sources)
    blank = jnp.zeros((1, width), jnp.bfloat16)
    send_tokens = jnp.concatenate([tokens, blank], 0)[inverse].reshape(
        peers, local_experts, capacity, width
    )
    send_grads = jnp.concatenate([cotangent, blank], 0)[inverse].reshape(
        peers, local_experts, capacity, width
    )
    arrived_tokens, arrived_grads = (
        lax.all_to_all(send_tokens, "expert", split_axis=0, concat_axis=0, tiled=True),
        lax.all_to_all(send_grads, "expert", split_axis=0, concat_axis=0, tiled=True),
    )
    full_in, full_down = (
        lax.all_gather(weight_in, "dp", axis=0, tiled=True),
        lax.all_gather(weight_down, "dp", axis=0, tiled=True),
    )
    gate_up = jnp.einsum(
        "secd,dei->seci", arrived_tokens, full_in, preferred_element_type=jnp.float32
    )
    hidden_grad = jnp.einsum(
        "secd,fed->secf", arrived_grads, full_down, preferred_element_type=jnp.float32
    )
    gate = gate_up[..., :hidden_units]
    upper = gate_up[..., hidden_units:]
    sigma = jax.nn.sigmoid(gate)
    grad_gate = hidden_grad * upper * sigma * (1.0 + gate * (1.0 - sigma))
    grad_up = hidden_grad * gate * sigma
    grad_mid = jnp.concatenate([grad_gate, grad_up], -1).astype(jnp.bfloat16)
    input_part = jnp.einsum("seci,dei->secd", grad_mid, full_in, preferred_element_type=jnp.float32)
    input_part = input_part.astype(jnp.bfloat16)
    returned = lax.all_to_all(
        input_part, "expert", split_axis=0, concat_axis=0, tiled=True
    ).reshape(experts * capacity, width)
    picked = returned[target].reshape(token_count, route_count, width)
    token_grad = jnp.sum(route_weights[:, :, None] * picked.astype(jnp.float32), axis=1).astype(
        jnp.bfloat16
    )
    grad_in = lax.psum_scatter(
        (
            jnp.einsum(
                "secd,seci->dei", arrived_tokens, grad_mid, preferred_element_type=jnp.float32
            )
            * grad_scale
        ).astype(jnp.bfloat16),
        "dp",
        scatter_dimension=0,
        tiled=True,
    )
    return (token_grad, grad_in)


LANES = 128
VMEM = 24 * 2**20
NT = (((1,), (1,)), ((), ()))
HIDE = 1 << 36
SMALL = 8 * 2**20
TN = (((0,), (0,)), ((), ()))


def payload_kernel(tokens, cotangent, ids, weights, out):
    count, width = tokens.shape
    out[:, :width] = tokens[...]
    out[:, width : 2 * width] = cotangent[...]
    lane = lax.broadcasted_iota(jnp.int32, (LANES, count), 0)
    n = LANES // 8
    total = jnp.zeros((LANES, count), jnp.float32)
    routed = jnp.zeros((LANES, count), jnp.float32)
    for k in range(ids.shape[0]):
        here = lane % n == ids[k : k + 1, :]
        total = total + jnp.where(here, weights[k : k + 1, :], 0.0)
        routed = routed + jnp.where(here, 1.0, 0.0)
    top = total.astype(jnp.bfloat16).astype(jnp.float32)
    rest = jnp.where(lane < 2 * n, total - top, jnp.where(lane < 3 * n, routed, 0.0))
    out[:, 2 * width :] = jnp.where(lane < n, top, rest).T.astype(jnp.bfloat16)


def payload_of(tokens, cotangent, ids, weights):
    count, width = tokens.shape
    return pl.pallas_call(
        payload_kernel,
        out_shape=jax.ShapeDtypeStruct((count, 2 * width + LANES), jnp.bfloat16),
        cost_estimate=pl.CostEstimate(flops=1 << 20, bytes_accessed=2 << 20, transcendentals=0),
        name="payload",
    )(tokens, cotangent, ids.T, weights.T)


def halves_kernel(place, weight, kept, given):
    quarter = weight.shape[2] // 4

    def part(k, out):
        for a in range(2):
            both = [weight[e, :, (2 * a + k) * quarter : (2 * a + k + 1) * quarter] for e in range(2)]
            out[:, 2 * a * quarter : 2 * (a + 1) * quarter] = jnp.concatenate(both, 1)

    for high in range(2):

        @pl.when(place[0] // 2 == high)
        def _():
            part(high, kept)
            part(1 - high, given)


def halves(place, weight):
    _, rows, cols = weight.shape
    vmem = pl.BlockSpec(memory_space=pltpu.VMEM)
    return pl.pallas_call(
        halves_kernel,
        in_specs=[pl.BlockSpec(memory_space=pltpu.SMEM), vmem],
        out_specs=[vmem] * 2,
        out_shape=[jax.ShapeDtypeStruct((rows, cols), jnp.bfloat16)] * 2,
        cost_estimate=pl.CostEstimate(flops=1 << 20, bytes_accessed=2 << 20, transcendentals=0),
        compiler_params=pltpu.CompilerParams(vmem_limit_bytes=SMALL),
        name="halves",
    )(place, weight)


def join_kernel(place, own, got, far, out):
    quarter = own.shape[1] // 4
    mine = (own[...].astype(jnp.float32) + got[...].astype(jnp.float32)).astype(jnp.bfloat16)

    def put(k, value):
        for a in range(2):
            for e in range(2):
                at = (2 * a + k) * quarter
                out[e, :, at : at + quarter] = value[:, (2 * a + e) * quarter : (2 * a + e + 1) * quarter]

    for high in range(2):

        @pl.when(place[0] // 2 == high)
        def _():
            put(high, mine)
            put(1 - high, far[...])


def join(place, own, got, far):
    vmem = pl.BlockSpec(memory_space=pltpu.VMEM)
    return pl.pallas_call(
        join_kernel,
        in_specs=[pl.BlockSpec(memory_space=pltpu.SMEM)] + [vmem] * 3,
        out_specs=vmem,
        out_shape=jax.ShapeDtypeStruct((2,) + own.shape, jnp.bfloat16),
        cost_estimate=pl.CostEstimate(flops=1 << 20, bytes_accessed=2 << 20, transcendentals=0),
        compiler_params=pltpu.CompilerParams(vmem_limit_bytes=SMALL),
        name="join",
    )(place, own, got, far)


def gather_weights(place, ws, ds, w_all, d_all, pick):
    rows, cols = ws[0].shape
    ff = ds[0].shape[0] // 2
    q, j = place[0], place[1]
    hidden = cols // 2
    for k, w in enumerate(ws):
        w_all[pl.ds(pl.multiple_of((q ^ k) * rows, rows), rows), :] = w[...]
    r = q % 2
    for e in range(2):
        d_all[pl.ds(pl.multiple_of((2 * e + r) * ff, ff), ff), :] = ds[0][pl.ds(e * ff, ff), :]
        d_all[pl.ds(pl.multiple_of((2 * e + 1 - r) * ff, ff), ff), :] = ds[1][pl.ds(e * ff, ff), :]
    lane = lax.broadcasted_iota(jnp.int32, (LANES, cols), 0)
    col = lax.broadcasted_iota(jnp.int32, (LANES, cols), 1)
    n = LANES // 8
    expert = 2 * j + jnp.where(col % hidden >= hidden // 2, 1, 0)
    first = jnp.where(col < hidden, expert, expert + 2 * n)
    second = jnp.where(col < hidden, expert + n, -1)
    hit = jnp.where(lane == first, 1.0, 0.0) + jnp.where(lane == second, 1.0, 0.0)
    pick[...] = hit.astype(jnp.bfloat16)


def grad_mid(xs, xo, w_all, d_all, pick, gm, gw):
    width, cols = w_all.shape
    hidden = cols // 2
    count = xs.shape[0] // 2
    for b in range(4):
        x = xs if b < 2 else xo
        at, to = pl.ds((b % 2) * count, count), pl.ds(b * count, count)
        gu = jnp.dot(x[at, :width], w_all[...], preferred_element_type=jnp.float32)
        dh = lax.dot_general(
            x[at, width : 2 * width], d_all[...], NT, preferred_element_type=jnp.float32
        )
        wm = jnp.dot(x[at, 2 * width :], pick[...], preferred_element_type=jnp.float32)
        w, on = wm[:, :hidden], wm[:, hidden:]
        gate, up = gu[:, :hidden], gu[:, hidden:]
        sg = 0.5 * jnp.tanh(0.5 * gate) + 0.5
        dhs = dh * on * sg
        gg = dhs * up * (1.0 + gate * (1.0 - sg))
        gup = dhs * gate
        gm[to, :hidden] = gg.astype(jnp.bfloat16)
        gm[to, hidden:] = gup.astype(jnp.bfloat16)
        gw[to, :hidden] = (gg * w).astype(jnp.bfloat16)
        gw[to, hidden:] = (gup * w).astype(jnp.bfloat16)


def weights_kernel(place, w0, w1, w2, w3, d0, d1, w_all, d_all, pick):
    gather_weights(place, (w0, w1, w2, w3), (d0, d1), w_all, d_all, pick)


def vmem_call(kernel, name, outs, *args, place=None, flops=HIDE):
    vmem = pl.BlockSpec(memory_space=pltpu.VMEM)
    specs = [vmem] * len(args)
    if place is not None:
        args, specs = (place, *args), [pl.BlockSpec(memory_space=pltpu.SMEM)] + specs
    return pl.pallas_call(
        kernel,
        in_specs=specs,
        out_specs=[vmem] * len(outs),
        out_shape=[jax.ShapeDtypeStruct(o, jnp.bfloat16) for o in outs],
        compiler_params=pltpu.CompilerParams(vmem_limit_bytes=VMEM),
        cost_estimate=pl.CostEstimate(flops=flops, bytes_accessed=12 << 20, transcendentals=0),
        name=name,
    )(*args)


def token_kernel(gw, w_all, ts, to):
    n = ts.shape[0]
    for b, out in enumerate((ts, to)):
        out[...] = lax.dot_general(
            gw[pl.ds(b * n, n), :], w_all[...], NT, preferred_element_type=jnp.float32
        ).astype(jnp.bfloat16)


def outer_kernel(scale, half, count, place, *refs):
    xs, gs, outs = refs[: 2 * half], refs[2 * half : 3 * half], refs[3 * half :]
    acc = None
    for k in range(half):
        x = jnp.concatenate([x[...] for x in xs[2 * k : 2 * k + 2]], 0)
        part = lax.dot_general(x, gs[k][...], TN, preferred_element_type=jnp.float32)
        acc = part if acc is None else acc + part
    value = (acc * scale).astype(jnp.bfloat16)
    for k in range(count):

        @pl.when(pl.program_id(0) == k)
        def _():
            outs[k][...] = value


def outer(place, xs, gs, scale, rows, top, count, flops=HIDE):
    cols = gs[0].shape[1]
    return pl.pallas_call(
        functools.partial(outer_kernel, scale, len(gs), count),
        grid_spec=pltpu.PrefetchScalarGridSpec(
            num_scalar_prefetch=1,
            grid=(count,),
            in_specs=[pl.BlockSpec((x.shape[0], rows), lambda i, s: (0, s[0] ^ (top - i))) for x in xs]
            + [pl.BlockSpec(g.shape, lambda i, s: (0, 0)) for g in gs],
            out_specs=[pl.BlockSpec((rows, cols), lambda i, s: (0, 0))] * count,
        ),
        out_shape=[jax.ShapeDtypeStruct((rows, cols), jnp.bfloat16)] * count,
        compiler_params=pltpu.CompilerParams(
            vmem_limit_bytes=VMEM, dimension_semantics=("arbitrary",)
        ),
        cost_estimate=pl.CostEstimate(flops=flops, bytes_accessed=12 << 20, transcendentals=0),
        name="outer",
    )(place, *xs, *gs)


def by_tokens(tokens, cotangent, expert_ids, route_weights, weight_in, weight_down):
    count, width = tokens.shape
    n_dp = lax.axis_size("dp")
    peers = lax.axis_size("expert")
    half = n_dp // 2
    rows, _, cols = weight_in.shape
    ff_rows = weight_down.shape[0]
    grad_scale = float(count * expert_ids.shape[1] * n_dp // weight_in.shape[1]) ** (-0.5)
    q = lax.axis_index("dp")
    place = jnp.stack([q, lax.axis_index("expert")]).astype(jnp.int32)
    across = [(i, (i + half) % n_dp) for i in range(n_dp)]
    beside = [(i, i ^ 1) for i in range(n_dp)]
    cores = [(i, i ^ 1) for i in range(peers)]
    hops = [[(i, i ^ (2 * m)) for i in range(peers)] for m in (1, 2, 3)]

    payload = payload_of(tokens, cotangent, expert_ids, route_weights)

    def spread(x):
        return [lax.ppermute(x, "expert", hop) for hop in hops]

    def plus(a, b):
        return (a.astype(jnp.float32) + b.astype(jnp.float32)).astype(jnp.bfloat16)

    after = lax.optimization_barrier

    near = [payload] + spread(payload)
    far_payload = lax.ppermute(payload, "dp", across)
    down1 = lax.ppermute(weight_down, "dp", beside)
    weight_in, payload = after((weight_in, payload))
    kept, given = halves(place, weight_in.swapaxes(0, 1))
    given, kept, far_payload = after((given, kept, far_payload))
    far = [far_payload] + spread(far_payload)
    w2 = lax.ppermute(given, "dp", across)
    w1 = lax.ppermute(kept, "dp", beside)
    downs = [d.swapaxes(0, 1).reshape(2 * ff_rows, width) for d in (weight_down, down1)]
    w2, w1, far[0] = after((w2, w1, far[0]))
    w3 = lax.ppermute(w2, "dp", beside)
    far_own = jnp.concatenate(far, 0)
    far_sib = lax.ppermute(far_own, "expert", cores)
    near_own = jnp.concatenate(near, 0)
    tall, wide = near_own.shape
    cols = kept.shape[1]
    mid_shape, token_shape = (2 * tall, cols), (tall, width)
    w_all, d_all, pick = vmem_call(
        weights_kernel,
        "weights",
        [(width, cols), (4 * ff_rows, width), (LANES, cols)],
        *(kept, w1, w2, w3, *downs),
        place=place,
    )
    far_sib, w_all, near_own = after((far_sib, w_all, near_own))
    near_sib = lax.ppermute(near_own, "expert", cores)

    def back_sums(own, got):
        return [plus(own[k * count : (k + 1) * count], got[k * count : (k + 1) * count]) for k in range(4)]

    def back_hops(sums):
        return [sums[0]] + [lax.ppermute(t, "expert", hop) for t, hop in zip(sums[1:], hops)]

    def mids(name, sib, own):
        return vmem_call(grad_mid, name, [mid_shape, mid_shape], sib, own, w_all, d_all, pick)

    def backs(name, gw):
        return vmem_call(
            token_kernel, name, [token_shape] * 2, gw, w_all, flops=4 * tall * cols * width
        )

    far_mid, far_gw = mids("far", far_sib, far_own)
    near_sib, far_mid = after((near_sib, far_mid))
    near_mid, near_gw = mids("near", near_sib, near_own)
    tiles = (far_sib, far_own, near_sib, near_own)
    (g3,) = outer(place, tiles, (far_mid, near_mid), grad_scale, rows, 3, 1)
    got3 = lax.ppermute(g3, "dp", beside)
    near_gw, g3 = after((near_gw, g3))
    near_ts, near_to = backs("near_tokens", near_gw)
    near_got = lax.ppermute(near_ts, "expert", cores)
    far_gw, near_to = after((far_gw, near_to))
    far_ts, far_to = backs("far_tokens", far_gw)
    far_got = lax.ppermute(far_ts, "expert", cores)
    near_mid, far_to = after((near_mid, far_to))
    g2, g1 = outer(place, tiles, (far_mid, near_mid), grad_scale, rows, 2, 2)
    got1 = lax.ppermute(g1, "dp", beside)
    far_got, near_got, g2 = after((far_got, near_got, g2))
    far_sums, near_sums = back_sums(far_to, far_got), back_sums(near_to, near_got)
    got3, *near_sums = after((got3, *near_sums))
    relay = plus(g2, got3)
    away_half = lax.ppermute(relay, "dp", across)
    near_mid, relay = after((near_mid, relay))
    (g0,) = outer(place, tiles, (far_mid, near_mid), grad_scale, rows, 0, 1, HIDE)
    g0, *far_sums = after((g0, *far_sums))
    far_back = back_hops(far_sums)
    away_half, got1, *far_back = after((away_half, got1, *far_back))
    away = sum(t.astype(jnp.float32) for t in far_back).astype(jnp.bfloat16)
    away, *near_sums = after((away, *near_sums))
    home = lax.ppermute(away, "dp", across)
    near_back = back_hops(near_sums)
    grad_in = join(place, g0, got1, away_half).swapaxes(0, 1)
    near_total = sum(t.astype(jnp.float32) for t in near_back)
    near_total, home = after((near_total, home))
    token_grad = (near_total + home.astype(jnp.float32)).astype(jnp.bfloat16)
    return token_grad, grad_in


def on_device(tokens, cotangent, expert_ids, route_weights, weight_in, weight_down):
    peers, n_dp = lax.axis_size("expert"), lax.axis_size("dp")
    experts = weight_in.shape[1] * peers
    capacity = 5 * tokens.shape[0] * expert_ids.shape[1] // (4 * experts)
    dense = weight_in.shape[1] * capacity >= tokens.shape[0]
    if dense and weight_in.shape[1] == 2 and n_dp == 4 and peers == 8 and experts == 16:
        form = by_tokens
    else:
        form = by_routes
    return form(tokens, cotangent, expert_ids, route_weights, weight_in, weight_down)


def solution(mesh):
    placed = (
        P(("dp", "expert"), None),
        P(("dp", "expert"), None),
        P(("dp", "expert"), None),
        P(("dp", "expert"), None),
        P("dp", "expert", None),
        P("dp", "expert", None),
    )
    return jax.shard_map(
        on_device,
        mesh=mesh,
        in_specs=placed,
        out_specs=(P(("dp", "expert"), None), P("dp", "expert", None)),
        check_vma=False,
    )
```

```python
import functools

import jax
import jax.numpy as jnp
from jax import lax
from jax.experimental import pallas as pl
from jax.experimental.pallas import tpu as pltpu
from jax.sharding import PartitionSpec as P


def by_routes(tokens, cotangent, expert_ids, route_weights, weight_in, weight_down):
    token_count = tokens.shape[0]
    width = tokens.shape[1]
    route_count = expert_ids.shape[1]
    peers = lax.axis_size("expert")
    local_experts = weight_in.shape[1]
    experts = local_experts * peers
    capacity = 5 * token_count * route_count // (4 * experts)
    hidden_units = weight_down.shape[0] * lax.axis_size("dp")
    rows_expert = token_count * route_count * lax.axis_size("dp") // local_experts
    grad_scale = float(rows_expert) ** (-0.5)
    flat_ids = expert_ids.reshape(-1)
    one_hot = (flat_ids[:, None] == jnp.arange(experts, dtype=jnp.int32)[None, :]).astype(jnp.int32)
    ranks = jnp.cumsum(one_hot, axis=0) - 1
    slots = jnp.sum(ranks * one_hot, axis=1)
    target = flat_ids * capacity + slots
    sources = jnp.arange(token_count * route_count, dtype=jnp.int32) // route_count
    inverse = jnp.full((experts * capacity,), token_count, jnp.int32).at[target].set(sources)
    blank = jnp.zeros((1, width), jnp.bfloat16)
    send_tokens = jnp.concatenate([tokens, blank], 0)[inverse].reshape(
        peers, local_experts, capacity, width
    )
    send_grads = jnp.concatenate([cotangent, blank], 0)[inverse].reshape(
        peers, local_experts, capacity, width
    )
    arrived_tokens, arrived_grads = (
        lax.all_to_all(send_tokens, "expert", split_axis=0, concat_axis=0, tiled=True),
        lax.all_to_all(send_grads, "expert", split_axis=0, concat_axis=0, tiled=True),
    )
    full_in, full_down = (
        lax.all_gather(weight_in, "dp", axis=0, tiled=True),
        lax.all_gather(weight_down, "dp", axis=0, tiled=True),
    )
    gate_up = jnp.einsum(
        "secd,dei->seci", arrived_tokens, full_in, preferred_element_type=jnp.float32
    )
    hidden_grad = jnp.einsum(
        "secd,fed->secf", arrived_grads, full_down, preferred_element_type=jnp.float32
    )
    gate = gate_up[..., :hidden_units]
    upper = gate_up[..., hidden_units:]
    sigma = jax.nn.sigmoid(gate)
    grad_gate = hidden_grad * upper * sigma * (1.0 + gate * (1.0 - sigma))
    grad_up = hidden_grad * gate * sigma
    grad_mid = jnp.concatenate([grad_gate, grad_up], -1).astype(jnp.bfloat16)
    input_part = jnp.einsum("seci,dei->secd", grad_mid, full_in, preferred_element_type=jnp.float32)
    input_part = input_part.astype(jnp.bfloat16)
    returned = lax.all_to_all(
        input_part, "expert", split_axis=0, concat_axis=0, tiled=True
    ).reshape(experts * capacity, width)
    picked = returned[target].reshape(token_count, route_count, width)
    token_grad = jnp.sum(route_weights[:, :, None] * picked.astype(jnp.float32), axis=1).astype(
        jnp.bfloat16
    )
    grad_in = lax.psum_scatter(
        (
            jnp.einsum(
                "secd,seci->dei", arrived_tokens, grad_mid, preferred_element_type=jnp.float32
            )
            * grad_scale
        ).astype(jnp.bfloat16),
        "dp",
        scatter_dimension=0,
        tiled=True,
    )
    return (token_grad, grad_in)


LANES = 128
VMEM = 24 * 2**20
NT = (((1,), (1,)), ((), ()))
HIDE = 1 << 36
SMALL = 8 * 2**20
TN = (((0,), (0,)), ((), ()))


def payload_kernel(tokens, cotangent, ids, weights, out):
    count, width = tokens.shape
    out[:, :width] = tokens[...]
    out[:, width : 2 * width] = cotangent[...]
    lane = lax.broadcasted_iota(jnp.int32, (LANES, count), 0)
    n = LANES // 8
    total = jnp.zeros((LANES, count), jnp.float32)
    routed = jnp.zeros((LANES, count), jnp.float32)
    for k in range(ids.shape[0]):
        here = lane % n == ids[k : k + 1, :]
        total = total + jnp.where(here, weights[k : k + 1, :], 0.0)
        routed = routed + jnp.where(here, 1.0, 0.0)
    top = total.astype(jnp.bfloat16).astype(jnp.float32)
    rest = jnp.where(lane < 2 * n, total - top, jnp.where(lane < 3 * n, routed, 0.0))
    out[:, 2 * width :] = jnp.where(lane < n, top, rest).T.astype(jnp.bfloat16)


def payload_of(tokens, cotangent, ids, weights):
    count, width = tokens.shape
    return pl.pallas_call(
        payload_kernel,
        out_shape=jax.ShapeDtypeStruct((count, 2 * width + LANES), jnp.bfloat16),
        cost_estimate=pl.CostEstimate(flops=1 << 20, bytes_accessed=2 << 20, transcendentals=0),
        name="payload",
    )(tokens, cotangent, ids.T, weights.T)


def halves_kernel(place, weight, kept, given):
    quarter = weight.shape[2] // 4

    def part(k, out):
        for a in range(2):
            both = [weight[e, :, (2 * a + k) * quarter : (2 * a + k + 1) * quarter] for e in range(2)]
            out[:, 2 * a * quarter : 2 * (a + 1) * quarter] = jnp.concatenate(both, 1)

    for high in range(2):

        @pl.when(place[0] // 2 == high)
        def _():
            part(high, kept)
            part(1 - high, given)


def halves(place, weight):
    _, rows, cols = weight.shape
    vmem = pl.BlockSpec(memory_space=pltpu.VMEM)
    return pl.pallas_call(
        halves_kernel,
        in_specs=[pl.BlockSpec(memory_space=pltpu.SMEM), vmem],
        out_specs=[vmem] * 2,
        out_shape=[jax.ShapeDtypeStruct((rows, cols), jnp.bfloat16)] * 2,
        cost_estimate=pl.CostEstimate(flops=1 << 20, bytes_accessed=2 << 20, transcendentals=0),
        compiler_params=pltpu.CompilerParams(vmem_limit_bytes=SMALL),
        name="halves",
    )(place, weight)


def join_kernel(place, own, got, far, out):
    quarter = own.shape[1] // 4
    mine = (own[...].astype(jnp.float32) + got[...].astype(jnp.float32)).astype(jnp.bfloat16)

    def put(k, value):
        for a in range(2):
            for e in range(2):
                at = (2 * a + k) * quarter
                out[e, :, at : at + quarter] = value[:, (2 * a + e) * quarter : (2 * a + e + 1) * quarter]

    for high in range(2):

        @pl.when(place[0] // 2 == high)
        def _():
            put(high, mine)
            put(1 - high, far[...])


def join(place, own, got, far):
    vmem = pl.BlockSpec(memory_space=pltpu.VMEM)
    return pl.pallas_call(
        join_kernel,
        in_specs=[pl.BlockSpec(memory_space=pltpu.SMEM)] + [vmem] * 3,
        out_specs=vmem,
        out_shape=jax.ShapeDtypeStruct((2,) + own.shape, jnp.bfloat16),
        cost_estimate=pl.CostEstimate(flops=1 << 20, bytes_accessed=2 << 20, transcendentals=0),
        compiler_params=pltpu.CompilerParams(vmem_limit_bytes=SMALL),
        name="join",
    )(place, own, got, far)


def gather_weights(place, ws, ds, w_all, d_all, pick):
    rows, cols = ws[0].shape
    ff = ds[0].shape[0] // 2
    q, j = place[0], place[1]
    hidden = cols // 2
    for k, w in enumerate(ws):
        w_all[pl.ds(pl.multiple_of((q ^ k) * rows, rows), rows), :] = w[...]
    r = q % 2
    for e in range(2):
        d_all[pl.ds(pl.multiple_of((2 * e + r) * ff, ff), ff), :] = ds[0][pl.ds(e * ff, ff), :]
        d_all[pl.ds(pl.multiple_of((2 * e + 1 - r) * ff, ff), ff), :] = ds[1][pl.ds(e * ff, ff), :]
    lane = lax.broadcasted_iota(jnp.int32, (LANES, cols), 0)
    col = lax.broadcasted_iota(jnp.int32, (LANES, cols), 1)
    n = LANES // 8
    expert = 2 * j + jnp.where(col % hidden >= hidden // 2, 1, 0)
    first = jnp.where(col < hidden, expert, expert + 2 * n)
    second = jnp.where(col < hidden, expert + n, -1)
    hit = jnp.where(lane == first, 1.0, 0.0) + jnp.where(lane == second, 1.0, 0.0)
    pick[...] = hit.astype(jnp.bfloat16)


def grad_mid(xs, xo, w_all, d_all, pick, gm, gw):
    width, cols = w_all.shape
    hidden = cols // 2
    count = xs.shape[0] // 2
    for b in range(4):
        x = xs if b < 2 else xo
        at, to = pl.ds((b % 2) * count, count), pl.ds(b * count, count)
        gu = jnp.dot(x[at, :width], w_all[...], preferred_element_type=jnp.float32)
        dh = lax.dot_general(
            x[at, width : 2 * width], d_all[...], NT, preferred_element_type=jnp.float32
        )
        wm = jnp.dot(x[at, 2 * width :], pick[...], preferred_element_type=jnp.float32)
        w, on = wm[:, :hidden], wm[:, hidden:]
        gate, up = gu[:, :hidden], gu[:, hidden:]
        sg = 0.5 * jnp.tanh(0.5 * gate) + 0.5
        dhs = dh * on * sg
        gg = dhs * up * (1.0 + gate * (1.0 - sg))
        gup = dhs * gate
        gm[to, :hidden] = gg.astype(jnp.bfloat16)
        gm[to, hidden:] = gup.astype(jnp.bfloat16)
        gw[to, :hidden] = (gg * w).astype(jnp.bfloat16)
        gw[to, hidden:] = (gup * w).astype(jnp.bfloat16)


def weights_kernel(place, w0, w1, w2, w3, d0, d1, w_all, d_all, pick):
    gather_weights(place, (w0, w1, w2, w3), (d0, d1), w_all, d_all, pick)


def vmem_call(kernel, name, outs, *args, place=None, flops=HIDE):
    vmem = pl.BlockSpec(memory_space=pltpu.VMEM)
    specs = [vmem] * len(args)
    if place is not None:
        args, specs = (place, *args), [pl.BlockSpec(memory_space=pltpu.SMEM)] + specs
    return pl.pallas_call(
        kernel,
        in_specs=specs,
        out_specs=[vmem] * len(outs),
        out_shape=[jax.ShapeDtypeStruct(o, jnp.bfloat16) for o in outs],
        compiler_params=pltpu.CompilerParams(vmem_limit_bytes=VMEM),
        cost_estimate=pl.CostEstimate(flops=flops, bytes_accessed=12 << 20, transcendentals=0),
        name=name,
    )(*args)


def token_kernel(gw, w_all, ts, to):
    n = ts.shape[0]
    for b, out in enumerate((ts, to)):
        out[...] = lax.dot_general(
            gw[pl.ds(b * n, n), :], w_all[...], NT, preferred_element_type=jnp.float32
        ).astype(jnp.bfloat16)


def outer_kernel(scale, half, count, place, *refs):
    xs, gs, outs = refs[: 2 * half], refs[2 * half : 3 * half], refs[3 * half :]
    acc = None
    for k in range(half):
        x = jnp.concatenate([x[...] for x in xs[2 * k : 2 * k + 2]], 0)
        part = lax.dot_general(x, gs[k][...], TN, preferred_element_type=jnp.float32)
        acc = part if acc is None else acc + part
    value = (acc * scale).astype(jnp.bfloat16)
    for k in range(count):

        @pl.when(pl.program_id(0) == k)
        def _():
            outs[k][...] = value


def outer(place, xs, gs, scale, rows, top, count, flops=HIDE):
    cols = gs[0].shape[1]
    return pl.pallas_call(
        functools.partial(outer_kernel, scale, len(gs), count),
        grid_spec=pltpu.PrefetchScalarGridSpec(
            num_scalar_prefetch=1,
            grid=(count,),
            in_specs=[pl.BlockSpec((x.shape[0], rows), lambda i, s: (0, s[0] ^ (top - i))) for x in xs]
            + [pl.BlockSpec(g.shape, lambda i, s: (0, 0)) for g in gs],
            out_specs=[pl.BlockSpec((rows, cols), lambda i, s: (0, 0))] * count,
        ),
        out_shape=[jax.ShapeDtypeStruct((rows, cols), jnp.bfloat16)] * count,
        compiler_params=pltpu.CompilerParams(
            vmem_limit_bytes=VMEM, dimension_semantics=("arbitrary",)
        ),
        cost_estimate=pl.CostEstimate(flops=flops, bytes_accessed=12 << 20, transcendentals=0),
        name="outer",
    )(place, *xs, *gs)


def by_tokens(tokens, cotangent, expert_ids, route_weights, weight_in, weight_down):
    count, width = tokens.shape
    n_dp = lax.axis_size("dp")
    peers = lax.axis_size("expert")
    half = n_dp // 2
    rows, _, cols = weight_in.shape
    ff_rows = weight_down.shape[0]
    grad_scale = float(count * expert_ids.shape[1] * n_dp // weight_in.shape[1]) ** (-0.5)
    q = lax.axis_index("dp")
    place = jnp.stack([q, lax.axis_index("expert")]).astype(jnp.int32)
    across = [(i, (i + half) % n_dp) for i in range(n_dp)]
    beside = [(i, i ^ 1) for i in range(n_dp)]
    cores = [(i, i ^ 1) for i in range(peers)]
    hops = [[(i, i ^ (2 * m)) for i in range(peers)] for m in (1, 2, 3)]

    payload = payload_of(tokens, cotangent, expert_ids, route_weights)

    def spread(x):
        return [lax.ppermute(x, "expert", hop) for hop in hops]

    def plus(a, b):
        return (a.astype(jnp.float32) + b.astype(jnp.float32)).astype(jnp.bfloat16)

    after = lax.optimization_barrier

    near = [payload] + spread(payload)
    far_payload = lax.ppermute(payload, "dp", across)
    down1 = lax.ppermute(weight_down, "dp", beside)
    weight_in, payload = after((weight_in, payload))
    kept, given = halves(place, weight_in.swapaxes(0, 1))
    given, kept, far_payload = after((given, kept, far_payload))
    far = [far_payload] + spread(far_payload)
    w2 = lax.ppermute(given, "dp", across)
    w1 = lax.ppermute(kept, "dp", beside)
    downs = [d.swapaxes(0, 1).reshape(2 * ff_rows, width) for d in (weight_down, down1)]
    w2, w1, far[0] = after((w2, w1, far[0]))
    w3 = lax.ppermute(w2, "dp", beside)
    far_own = jnp.concatenate(far, 0)
    far_sib = lax.ppermute(far_own, "expert", cores)
    near_own = jnp.concatenate(near, 0)
    tall, wide = near_own.shape
    cols = kept.shape[1]
    mid_shape, token_shape = (2 * tall, cols), (tall, width)
    w_all, d_all, pick = vmem_call(
        weights_kernel,
        "weights",
        [(width, cols), (4 * ff_rows, width), (LANES, cols)],
        *(kept, w1, w2, w3, *downs),
        place=place,
    )
    far_sib, w_all, near_own = after((far_sib, w_all, near_own))
    near_sib = lax.ppermute(near_own, "expert", cores)

    def back_sums(own, got):
        return [plus(own[k * count : (k + 1) * count], got[k * count : (k + 1) * count]) for k in range(4)]

    def back_hops(sums):
        return [sums[0]] + [lax.ppermute(t, "expert", hop) for t, hop in zip(sums[1:], hops)]

    def mids(name, sib, own):
        return vmem_call(grad_mid, name, [mid_shape, mid_shape], sib, own, w_all, d_all, pick)

    def backs(name, gw, flops):
        return vmem_call(token_kernel, name, [token_shape] * 2, gw, w_all, flops=flops)

    far_mid, far_gw = mids("far", far_sib, far_own)
    near_sib, far_mid = after((near_sib, far_mid))
    near_mid, near_gw = mids("near", near_sib, near_own)
    tiles = (far_sib, far_own, near_sib, near_own)
    (g3,) = outer(place, tiles, (far_mid, near_mid), grad_scale, rows, 3, 1)
    got3 = lax.ppermute(g3, "dp", beside)
    far_gw, g3 = after((far_gw, g3))
    far_ts, far_to = backs("far_tokens", far_gw, 1 << 20)
    far_got = lax.ppermute(far_ts, "expert", cores)
    near_mid, far_to = after((near_mid, far_to))
    g2, g1 = outer(place, tiles, (far_mid, near_mid), grad_scale, rows, 2, 2)
    got1 = lax.ppermute(g1, "dp", beside)
    far_got, g2 = after((far_got, g2))
    far_sums = back_sums(far_to, far_got)
    far_back = back_hops(far_sums)
    got3, *far_sums = after((got3, *far_sums))
    relay = plus(g2, got3)
    away_half = lax.ppermute(relay, "dp", across)
    near_gw, relay = after((near_gw, relay))
    near_ts, near_to = backs("near_tokens", near_gw, HIDE)
    near_got = lax.ppermute(near_ts, "expert", cores)
    near_mid, near_to, *far_back = after((near_mid, near_to, *far_back))
    (g0,) = outer(place, tiles, (far_mid, near_mid), grad_scale, rows, 0, 1)
    near_got, g0 = after((near_got, g0))
    near_sums = back_sums(near_to, near_got)
    away = sum(t.astype(jnp.float32) for t in far_back).astype(jnp.bfloat16)
    away, *near_sums = after((away, *near_sums))
    home = lax.ppermute(away, "dp", across)
    near_back = back_hops(near_sums)
    grad_in = join(place, g0, got1, away_half).swapaxes(0, 1)
    near_total = sum(t.astype(jnp.float32) for t in near_back)
    near_total, home = after((near_total, home))
    token_grad = (near_total + home.astype(jnp.float32)).astype(jnp.bfloat16)
    return token_grad, grad_in


def on_device(tokens, cotangent, expert_ids, route_weights, weight_in, weight_down):
    peers, n_dp = lax.axis_size("expert"), lax.axis_size("dp")
    experts = weight_in.shape[1] * peers
    capacity = 5 * tokens.shape[0] * expert_ids.shape[1] // (4 * experts)
    dense = weight_in.shape[1] * capacity >= tokens.shape[0]
    if dense and weight_in.shape[1] == 2 and n_dp == 4 and peers == 8 and experts == 16:
        form = by_tokens
    else:
        form = by_routes
    return form(tokens, cotangent, expert_ids, route_weights, weight_in, weight_down)


def solution(mesh):
    placed = (
        P(("dp", "expert"), None),
        P(("dp", "expert"), None),
        P(("dp", "expert"), None),
        P(("dp", "expert"), None),
        P("dp", "expert", None),
        P("dp", "expert", None),
    )
    return jax.shard_map(
        on_device,
        mesh=mesh,
        in_specs=placed,
        out_specs=(P(("dp", "expert"), None), P("dp", "expert", None)),
        check_vma=False,
    )
```

```python
import functools

import jax
import jax.numpy as jnp
from jax import lax
from jax.experimental import pallas as pl
from jax.experimental.pallas import tpu as pltpu
from jax.sharding import PartitionSpec as P


def by_routes(tokens, cotangent, expert_ids, route_weights, weight_in, weight_down):
    token_count = tokens.shape[0]
    width = tokens.shape[1]
    route_count = expert_ids.shape[1]
    peers = lax.axis_size("expert")
    local_experts = weight_in.shape[1]
    experts = local_experts * peers
    capacity = 5 * token_count * route_count // (4 * experts)
    hidden_units = weight_down.shape[0] * lax.axis_size("dp")
    rows_expert = token_count * route_count * lax.axis_size("dp") // local_experts
    grad_scale = float(rows_expert) ** (-0.5)
    flat_ids = expert_ids.reshape(-1)
    one_hot = (flat_ids[:, None] == jnp.arange(experts, dtype=jnp.int32)[None, :]).astype(jnp.int32)
    ranks = jnp.cumsum(one_hot, axis=0) - 1
    slots = jnp.sum(ranks * one_hot, axis=1)
    target = flat_ids * capacity + slots
    sources = jnp.arange(token_count * route_count, dtype=jnp.int32) // route_count
    inverse = jnp.full((experts * capacity,), token_count, jnp.int32).at[target].set(sources)
    blank = jnp.zeros((1, width), jnp.bfloat16)
    send_tokens = jnp.concatenate([tokens, blank], 0)[inverse].reshape(
        peers, local_experts, capacity, width
    )
    send_grads = jnp.concatenate([cotangent, blank], 0)[inverse].reshape(
        peers, local_experts, capacity, width
    )
    arrived_tokens, arrived_grads = (
        lax.all_to_all(send_tokens, "expert", split_axis=0, concat_axis=0, tiled=True),
        lax.all_to_all(send_grads, "expert", split_axis=0, concat_axis=0, tiled=True),
    )
    full_in, full_down = (
        lax.all_gather(weight_in, "dp", axis=0, tiled=True),
        lax.all_gather(weight_down, "dp", axis=0, tiled=True),
    )
    gate_up = jnp.einsum(
        "secd,dei->seci", arrived_tokens, full_in, preferred_element_type=jnp.float32
    )
    hidden_grad = jnp.einsum(
        "secd,fed->secf", arrived_grads, full_down, preferred_element_type=jnp.float32
    )
    gate = gate_up[..., :hidden_units]
    upper = gate_up[..., hidden_units:]
    sigma = jax.nn.sigmoid(gate)
    grad_gate = hidden_grad * upper * sigma * (1.0 + gate * (1.0 - sigma))
    grad_up = hidden_grad * gate * sigma
    grad_mid = jnp.concatenate([grad_gate, grad_up], -1).astype(jnp.bfloat16)
    input_part = jnp.einsum("seci,dei->secd", grad_mid, full_in, preferred_element_type=jnp.float32)
    input_part = input_part.astype(jnp.bfloat16)
    returned = lax.all_to_all(
        input_part, "expert", split_axis=0, concat_axis=0, tiled=True
    ).reshape(experts * capacity, width)
    picked = returned[target].reshape(token_count, route_count, width)
    token_grad = jnp.sum(route_weights[:, :, None] * picked.astype(jnp.float32), axis=1).astype(
        jnp.bfloat16
    )
    grad_in = lax.psum_scatter(
        (
            jnp.einsum(
                "secd,seci->dei", arrived_tokens, grad_mid, preferred_element_type=jnp.float32
            )
            * grad_scale
        ).astype(jnp.bfloat16),
        "dp",
        scatter_dimension=0,
        tiled=True,
    )
    return (token_grad, grad_in)


LANES = 128
VMEM = 24 * 2**20
NT = (((1,), (1,)), ((), ()))
HIDE = 1 << 36
SMALL = 8 * 2**20
TN = (((0,), (0,)), ((), ()))


def payload_kernel(tokens, cotangent, ids, weights, out):
    count, width = tokens.shape
    out[:, :width] = tokens[...]
    out[:, width : 2 * width] = cotangent[...]
    lane = lax.broadcasted_iota(jnp.int32, (LANES, count), 0)
    n = LANES // 8
    total = jnp.zeros((LANES, count), jnp.float32)
    routed = jnp.zeros((LANES, count), jnp.float32)
    for k in range(ids.shape[0]):
        here = lane % n == ids[k : k + 1, :]
        total = total + jnp.where(here, weights[k : k + 1, :], 0.0)
        routed = routed + jnp.where(here, 1.0, 0.0)
    top = total.astype(jnp.bfloat16).astype(jnp.float32)
    rest = jnp.where(lane < 2 * n, total - top, jnp.where(lane < 3 * n, routed, 0.0))
    out[:, 2 * width :] = jnp.where(lane < n, top, rest).T.astype(jnp.bfloat16)


def payload_of(tokens, cotangent, ids, weights):
    count, width = tokens.shape
    return pl.pallas_call(
        payload_kernel,
        out_shape=jax.ShapeDtypeStruct((count, 2 * width + LANES), jnp.bfloat16),
        cost_estimate=pl.CostEstimate(flops=1 << 20, bytes_accessed=2 << 20, transcendentals=0),
        name="payload",
    )(tokens, cotangent, ids.T, weights.T)


def halves_kernel(place, weight, kept, given):
    quarter = weight.shape[2] // 4

    def part(k, out):
        for a in range(2):
            both = [weight[e, :, (2 * a + k) * quarter : (2 * a + k + 1) * quarter] for e in range(2)]
            out[:, 2 * a * quarter : 2 * (a + 1) * quarter] = jnp.concatenate(both, 1)

    for high in range(2):

        @pl.when(place[0] // 2 == high)
        def _():
            part(high, kept)
            part(1 - high, given)


def halves(place, weight):
    _, rows, cols = weight.shape
    vmem = pl.BlockSpec(memory_space=pltpu.VMEM)
    return pl.pallas_call(
        halves_kernel,
        in_specs=[pl.BlockSpec(memory_space=pltpu.SMEM), vmem],
        out_specs=[vmem] * 2,
        out_shape=[jax.ShapeDtypeStruct((rows, cols), jnp.bfloat16)] * 2,
        cost_estimate=pl.CostEstimate(flops=1 << 20, bytes_accessed=2 << 20, transcendentals=0),
        compiler_params=pltpu.CompilerParams(vmem_limit_bytes=SMALL),
        name="halves",
    )(place, weight)


def join_kernel(place, own, got, far, out):
    quarter = own.shape[1] // 4
    mine = (own[...].astype(jnp.float32) + got[...].astype(jnp.float32)).astype(jnp.bfloat16)

    def put(k, value):
        for a in range(2):
            for e in range(2):
                at = (2 * a + k) * quarter
                out[e, :, at : at + quarter] = value[:, (2 * a + e) * quarter : (2 * a + e + 1) * quarter]

    for high in range(2):

        @pl.when(place[0] // 2 == high)
        def _():
            put(high, mine)
            put(1 - high, far[...])


def join(place, own, got, far):
    vmem = pl.BlockSpec(memory_space=pltpu.VMEM)
    return pl.pallas_call(
        join_kernel,
        in_specs=[pl.BlockSpec(memory_space=pltpu.SMEM)] + [vmem] * 3,
        out_specs=vmem,
        out_shape=jax.ShapeDtypeStruct((2,) + own.shape, jnp.bfloat16),
        cost_estimate=pl.CostEstimate(flops=1 << 20, bytes_accessed=2 << 20, transcendentals=0),
        compiler_params=pltpu.CompilerParams(vmem_limit_bytes=SMALL),
        name="join",
    )(place, own, got, far)


def gather_weights(place, ws, ds, w_all, d_all, pick):
    rows, cols = ws[0].shape
    ff = ds[0].shape[0] // 2
    q, j = place[0], place[1]
    hidden = cols // 2
    for k, w in enumerate(ws):
        w_all[pl.ds(pl.multiple_of((q ^ k) * rows, rows), rows), :] = w[...]
    r = q % 2
    for e in range(2):
        d_all[pl.ds(pl.multiple_of((2 * e + r) * ff, ff), ff), :] = ds[0][pl.ds(e * ff, ff), :]
        d_all[pl.ds(pl.multiple_of((2 * e + 1 - r) * ff, ff), ff), :] = ds[1][pl.ds(e * ff, ff), :]
    lane = lax.broadcasted_iota(jnp.int32, (LANES, cols), 0)
    col = lax.broadcasted_iota(jnp.int32, (LANES, cols), 1)
    n = LANES // 8
    expert = 2 * j + jnp.where(col % hidden >= hidden // 2, 1, 0)
    first = jnp.where(col < hidden, expert, expert + 2 * n)
    second = jnp.where(col < hidden, expert + n, -1)
    hit = jnp.where(lane == first, 1.0, 0.0) + jnp.where(lane == second, 1.0, 0.0)
    pick[...] = hit.astype(jnp.bfloat16)


def grad_mid(xs, xo, w_all, d_all, pick, gm, gw):
    width, cols = w_all.shape
    hidden = cols // 2
    count = xs.shape[0] // 2
    for b in range(4):
        x = xs if b < 2 else xo
        at, to = pl.ds((b % 2) * count, count), pl.ds(b * count, count)
        gu = jnp.dot(x[at, :width], w_all[...], preferred_element_type=jnp.float32)
        dh = lax.dot_general(
            x[at, width : 2 * width], d_all[...], NT, preferred_element_type=jnp.float32
        )
        wm = jnp.dot(x[at, 2 * width :], pick[...], preferred_element_type=jnp.float32)
        w, on = wm[:, :hidden], wm[:, hidden:]
        gate, up = gu[:, :hidden], gu[:, hidden:]
        sg = 0.5 * jnp.tanh(0.5 * gate) + 0.5
        dhs = dh * on * sg
        gg = dhs * up * (1.0 + gate * (1.0 - sg))
        gup = dhs * gate
        gm[to, :hidden] = gg.astype(jnp.bfloat16)
        gm[to, hidden:] = gup.astype(jnp.bfloat16)
        gw[to, :hidden] = (gg * w).astype(jnp.bfloat16)
        gw[to, hidden:] = (gup * w).astype(jnp.bfloat16)


def weights_kernel(place, w0, w1, w2, w3, d0, d1, w_all, d_all, pick):
    gather_weights(place, (w0, w1, w2, w3), (d0, d1), w_all, d_all, pick)


def vmem_call(kernel, name, outs, *args, place=None, flops=HIDE):
    vmem = pl.BlockSpec(memory_space=pltpu.VMEM)
    specs = [vmem] * len(args)
    if place is not None:
        args, specs = (place, *args), [pl.BlockSpec(memory_space=pltpu.SMEM)] + specs
    return pl.pallas_call(
        kernel,
        in_specs=specs,
        out_specs=[vmem] * len(outs),
        out_shape=[jax.ShapeDtypeStruct(o, jnp.bfloat16) for o in outs],
        compiler_params=pltpu.CompilerParams(vmem_limit_bytes=VMEM),
        cost_estimate=pl.CostEstimate(flops=flops, bytes_accessed=12 << 20, transcendentals=0),
        name=name,
    )(*args)


def token_kernel(gw, w_all, ts, to):
    n = ts.shape[0]
    for b, out in enumerate((ts, to)):
        out[...] = lax.dot_general(
            gw[pl.ds(b * n, n), :], w_all[...], NT, preferred_element_type=jnp.float32
        ).astype(jnp.bfloat16)


def outer_kernel(scale, half, count, place, *refs):
    xs, gs, outs = refs[: 2 * half], refs[2 * half : 3 * half], refs[3 * half :]
    acc = None
    for k in range(half):
        x = jnp.concatenate([x[...] for x in xs[2 * k : 2 * k + 2]], 0)
        part = lax.dot_general(x, gs[k][...], TN, preferred_element_type=jnp.float32)
        acc = part if acc is None else acc + part
    value = (acc * scale).astype(jnp.bfloat16)
    for k in range(count):

        @pl.when(pl.program_id(0) == k)
        def _():
            outs[k][...] = value


def outer(place, xs, gs, scale, rows, top, count, flops=HIDE):
    cols = gs[0].shape[1]
    return pl.pallas_call(
        functools.partial(outer_kernel, scale, len(gs), count),
        grid_spec=pltpu.PrefetchScalarGridSpec(
            num_scalar_prefetch=1,
            grid=(count,),
            in_specs=[pl.BlockSpec((x.shape[0], rows), lambda i, s: (0, s[0] ^ (top - i))) for x in xs]
            + [pl.BlockSpec(g.shape, lambda i, s: (0, 0)) for g in gs],
            out_specs=[pl.BlockSpec((rows, cols), lambda i, s: (0, 0))] * count,
        ),
        out_shape=[jax.ShapeDtypeStruct((rows, cols), jnp.bfloat16)] * count,
        compiler_params=pltpu.CompilerParams(
            vmem_limit_bytes=VMEM, dimension_semantics=("arbitrary",)
        ),
        cost_estimate=pl.CostEstimate(flops=flops, bytes_accessed=12 << 20, transcendentals=0),
        name="outer",
    )(place, *xs, *gs)


def by_tokens(tokens, cotangent, expert_ids, route_weights, weight_in, weight_down):
    count, width = tokens.shape
    n_dp = lax.axis_size("dp")
    peers = lax.axis_size("expert")
    half = n_dp // 2
    rows, _, cols = weight_in.shape
    ff_rows = weight_down.shape[0]
    grad_scale = float(count * expert_ids.shape[1] * n_dp // weight_in.shape[1]) ** (-0.5)
    q = lax.axis_index("dp")
    place = jnp.stack([q, lax.axis_index("expert")]).astype(jnp.int32)
    across = [(i, (i + half) % n_dp) for i in range(n_dp)]
    beside = [(i, i ^ 1) for i in range(n_dp)]
    cores = [(i, i ^ 1) for i in range(peers)]
    hops = [[(i, i ^ (2 * m)) for i in range(peers)] for m in (1, 2, 3)]

    payload = payload_of(tokens, cotangent, expert_ids, route_weights)

    def spread(x):
        return [lax.ppermute(x, "expert", hop) for hop in hops]

    def plus(a, b):
        return (a.astype(jnp.float32) + b.astype(jnp.float32)).astype(jnp.bfloat16)

    after = lax.optimization_barrier

    near = [payload] + spread(payload)
    far_payload = lax.ppermute(payload, "dp", across)
    down1 = lax.ppermute(weight_down, "dp", beside)
    weight_in, payload = after((weight_in, payload))
    kept, given = halves(place, weight_in.swapaxes(0, 1))
    given, kept, far_payload = after((given, kept, far_payload))
    far = [far_payload] + spread(far_payload)
    w2 = lax.ppermute(given, "dp", across)
    w1 = lax.ppermute(kept, "dp", beside)
    downs = [d.swapaxes(0, 1).reshape(2 * ff_rows, width) for d in (weight_down, down1)]
    w2, w1, far[0] = after((w2, w1, far[0]))
    w3 = lax.ppermute(w2, "dp", beside)
    far_own = jnp.concatenate(far, 0)
    far_sib = lax.ppermute(far_own, "expert", cores)
    near_own = jnp.concatenate(near, 0)
    tall, wide = near_own.shape
    cols = kept.shape[1]
    mid_shape, token_shape = (2 * tall, cols), (tall, width)
    w_all, d_all, pick = vmem_call(
        weights_kernel,
        "weights",
        [(width, cols), (4 * ff_rows, width), (LANES, cols)],
        *(kept, w1, w2, w3, *downs),
        place=place,
    )
    far_sib, w_all, near_own = after((far_sib, w_all, near_own))
    near_sib = lax.ppermute(near_own, "expert", cores)

    def back_sums(own, got):
        return [plus(own[k * count : (k + 1) * count], got[k * count : (k + 1) * count]) for k in range(4)]

    def back_hops(sums):
        return [sums[0]] + [lax.ppermute(t, "expert", hop) for t, hop in zip(sums[1:], hops)]

    def mids(name, sib, own):
        return vmem_call(grad_mid, name, [mid_shape, mid_shape], sib, own, w_all, d_all, pick)

    def backs(name, gw, flops):
        return vmem_call(token_kernel, name, [token_shape] * 2, gw, w_all, flops=flops)

    far_mid, far_gw = mids("far", far_sib, far_own)
    near_sib, far_mid = after((near_sib, far_mid))
    near_mid, near_gw = mids("near", near_sib, near_own)
    tiles = (far_sib, far_own, near_sib, near_own)
    (g3,) = outer(place, tiles, (far_mid, near_mid), grad_scale, rows, 3, 1)
    got3 = lax.ppermute(g3, "dp", beside)
    far_gw, g3 = after((far_gw, g3))
    far_ts, far_to = backs("far_tokens", far_gw, 1 << 20)
    far_got = lax.ppermute(far_ts, "expert", cores)
    near_mid, far_to = after((near_mid, far_to))
    g2, g1 = outer(place, tiles, (far_mid, near_mid), grad_scale, rows, 2, 2)
    got1 = lax.ppermute(g1, "dp", beside)
    far_got, g2 = after((far_got, g2))
    far_sums = back_sums(far_to, far_got)
    far_back = back_hops(far_sums)
    got3, *far_sums = after((got3, *far_sums))
    relay = plus(g2, got3)
    away_half = lax.ppermute(relay, "dp", across)
    near_gw, relay = after((near_gw, relay))
    near_ts, near_to = backs("near_tokens", near_gw, 1 << 20)
    near_got = lax.ppermute(near_ts, "expert", cores)
    near_mid, near_to, *far_back = after((near_mid, near_to, *far_back))
    (g0,) = outer(place, tiles, (far_mid, near_mid), grad_scale, rows, 0, 1)
    near_got, g0 = after((near_got, g0))
    near_sums = back_sums(near_to, near_got)
    away = sum(t.astype(jnp.float32) for t in far_back).astype(jnp.bfloat16)
    away, *near_sums = after((away, *near_sums))
    home = lax.ppermute(away, "dp", across)
    near_back = back_hops(near_sums)
    grad_in = join(place, g0, got1, away_half).swapaxes(0, 1)
    near_total = sum(t.astype(jnp.float32) for t in near_back)
    near_total, home = after((near_total, home))
    token_grad = (near_total + home.astype(jnp.float32)).astype(jnp.bfloat16)
    return token_grad, grad_in


def on_device(tokens, cotangent, expert_ids, route_weights, weight_in, weight_down):
    peers, n_dp = lax.axis_size("expert"), lax.axis_size("dp")
    experts = weight_in.shape[1] * peers
    capacity = 5 * tokens.shape[0] * expert_ids.shape[1] // (4 * experts)
    dense = weight_in.shape[1] * capacity >= tokens.shape[0]
    if dense and weight_in.shape[1] == 2 and n_dp == 4 and peers == 8 and experts == 16:
        form = by_tokens
    else:
        form = by_routes
    return form(tokens, cotangent, expert_ids, route_weights, weight_in, weight_down)


def solution(mesh):
    placed = (
        P(("dp", "expert"), None),
        P(("dp", "expert"), None),
        P(("dp", "expert"), None),
        P(("dp", "expert"), None),
        P("dp", "expert", None),
        P("dp", "expert", None),
    )
    return jax.shard_map(
        on_device,
        mesh=mesh,
        in_specs=placed,
        out_specs=(P(("dp", "expert"), None), P("dp", "expert", None)),
        check_vma=False,
    )
```

```python
import functools

import jax
import jax.numpy as jnp
from jax import lax
from jax.experimental import pallas as pl
from jax.experimental.pallas import tpu as pltpu
from jax.sharding import PartitionSpec as P


def by_routes(tokens, cotangent, expert_ids, route_weights, weight_in, weight_down):
    token_count = tokens.shape[0]
    width = tokens.shape[1]
    route_count = expert_ids.shape[1]
    peers = lax.axis_size("expert")
    local_experts = weight_in.shape[1]
    experts = local_experts * peers
    capacity = 5 * token_count * route_count // (4 * experts)
    hidden_units = weight_down.shape[0] * lax.axis_size("dp")
    rows_expert = token_count * route_count * lax.axis_size("dp") // local_experts
    grad_scale = float(rows_expert) ** (-0.5)
    flat_ids = expert_ids.reshape(-1)
    one_hot = (flat_ids[:, None] == jnp.arange(experts, dtype=jnp.int32)[None, :]).astype(jnp.int32)
    ranks = jnp.cumsum(one_hot, axis=0) - 1
    slots = jnp.sum(ranks * one_hot, axis=1)
    target = flat_ids * capacity + slots
    sources = jnp.arange(token_count * route_count, dtype=jnp.int32) // route_count
    inverse = jnp.full((experts * capacity,), token_count, jnp.int32).at[target].set(sources)
    blank = jnp.zeros((1, width), jnp.bfloat16)
    send_tokens = jnp.concatenate([tokens, blank], 0)[inverse].reshape(
        peers, local_experts, capacity, width
    )
    send_grads = jnp.concatenate([cotangent, blank], 0)[inverse].reshape(
        peers, local_experts, capacity, width
    )
    arrived_tokens, arrived_grads = (
        lax.all_to_all(send_tokens, "expert", split_axis=0, concat_axis=0, tiled=True),
        lax.all_to_all(send_grads, "expert", split_axis=0, concat_axis=0, tiled=True),
    )
    full_in, full_down = (
        lax.all_gather(weight_in, "dp", axis=0, tiled=True),
        lax.all_gather(weight_down, "dp", axis=0, tiled=True),
    )
    gate_up = jnp.einsum(
        "secd,dei->seci", arrived_tokens, full_in, preferred_element_type=jnp.float32
    )
    hidden_grad = jnp.einsum(
        "secd,fed->secf", arrived_grads, full_down, preferred_element_type=jnp.float32
    )
    gate = gate_up[..., :hidden_units]
    upper = gate_up[..., hidden_units:]
    sigma = jax.nn.sigmoid(gate)
    grad_gate = hidden_grad * upper * sigma * (1.0 + gate * (1.0 - sigma))
    grad_up = hidden_grad * gate * sigma
    grad_mid = jnp.concatenate([grad_gate, grad_up], -1).astype(jnp.bfloat16)
    input_part = jnp.einsum("seci,dei->secd", grad_mid, full_in, preferred_element_type=jnp.float32)
    input_part = input_part.astype(jnp.bfloat16)
    returned = lax.all_to_all(
        input_part, "expert", split_axis=0, concat_axis=0, tiled=True
    ).reshape(experts * capacity, width)
    picked = returned[target].reshape(token_count, route_count, width)
    token_grad = jnp.sum(route_weights[:, :, None] * picked.astype(jnp.float32), axis=1).astype(
        jnp.bfloat16
    )
    grad_in = lax.psum_scatter(
        (
            jnp.einsum(
                "secd,seci->dei", arrived_tokens, grad_mid, preferred_element_type=jnp.float32
            )
            * grad_scale
        ).astype(jnp.bfloat16),
        "dp",
        scatter_dimension=0,
        tiled=True,
    )
    return (token_grad, grad_in)


LANES = 128
VMEM = 24 * 2**20
NT = (((1,), (1,)), ((), ()))
HIDE = 1 << 36
SMALL = 8 * 2**20
TN = (((0,), (0,)), ((), ()))


def payload_kernel(tokens, cotangent, ids, weights, out, meta, sems):
    count, width = tokens.shape
    copies = [
        pltpu.make_async_copy(tokens, out.at[:, pl.ds(0, width)], sems.at[0]),
        pltpu.make_async_copy(cotangent, out.at[:, pl.ds(width, width)], sems.at[1]),
        pltpu.make_async_copy(meta, out.at[:, pl.ds(2 * width, LANES)], sems.at[2]),
    ]
    copies[0].start()
    copies[1].start()
    lane = lax.broadcasted_iota(jnp.int32, (LANES, count), 0)
    n = LANES // 8
    total = jnp.zeros((LANES, count), jnp.float32)
    routed = jnp.zeros((LANES, count), jnp.float32)
    for k in range(ids.shape[0]):
        here = lane % n == ids[k : k + 1, :]
        total = total + jnp.where(here, weights[k : k + 1, :], 0.0)
        routed = routed + jnp.where(here, 1.0, 0.0)
    top = total.astype(jnp.bfloat16).astype(jnp.float32)
    rest = jnp.where(lane < 2 * n, total - top, jnp.where(lane < 3 * n, routed, 0.0))
    meta[...] = jnp.where(lane < n, top, rest).T.astype(jnp.bfloat16)
    copies[2].start()
    for copy in copies:
        copy.wait()


def payload_of(tokens, cotangent, ids, weights):
    count, width = tokens.shape
    return pl.pallas_call(
        payload_kernel,
        in_specs=[pl.BlockSpec(memory_space=pl.ANY)] * 2 + [pl.BlockSpec(memory_space=pltpu.VMEM)] * 2,
        out_specs=pl.BlockSpec(memory_space=pl.ANY),
        scratch_shapes=[pltpu.VMEM((count, LANES), jnp.bfloat16), pltpu.SemaphoreType.DMA((3,))],
        out_shape=jax.ShapeDtypeStruct((count, 2 * width + LANES), jnp.bfloat16),
        cost_estimate=pl.CostEstimate(flops=1 << 20, bytes_accessed=2 << 20, transcendentals=0),
        compiler_params=pltpu.CompilerParams(vmem_limit_bytes=60 * 2**20),
        name="payload",
    )(tokens, cotangent, ids.T, weights.T)


def halves_kernel(place, weight, kept, given):
    quarter = weight.shape[2] // 4

    def part(k, out):
        for a in range(2):
            both = [weight[e, :, (2 * a + k) * quarter : (2 * a + k + 1) * quarter] for e in range(2)]
            out[:, 2 * a * quarter : 2 * (a + 1) * quarter] = jnp.concatenate(both, 1)

    for high in range(2):

        @pl.when(place[0] // 2 == high)
        def _():
            part(high, kept)
            part(1 - high, given)


def halves(place, weight):
    _, rows, cols = weight.shape
    vmem = pl.BlockSpec(memory_space=pltpu.VMEM)
    return pl.pallas_call(
        halves_kernel,
        in_specs=[pl.BlockSpec(memory_space=pltpu.SMEM), vmem],
        out_specs=[vmem] * 2,
        out_shape=[jax.ShapeDtypeStruct((rows, cols), jnp.bfloat16)] * 2,
        cost_estimate=pl.CostEstimate(flops=1 << 20, bytes_accessed=2 << 20, transcendentals=0),
        compiler_params=pltpu.CompilerParams(vmem_limit_bytes=SMALL),
        name="halves",
    )(place, weight)


def join_kernel(place, own, got, far, out):
    quarter = own.shape[1] // 4
    mine = (own[...].astype(jnp.float32) + got[...].astype(jnp.float32)).astype(jnp.bfloat16)

    def put(k, value):
        for a in range(2):
            for e in range(2):
                at = (2 * a + k) * quarter
                out[e, :, at : at + quarter] = value[:, (2 * a + e) * quarter : (2 * a + e + 1) * quarter]

    for high in range(2):

        @pl.when(place[0] // 2 == high)
        def _():
            put(high, mine)
            put(1 - high, far[...])


def join(place, own, got, far):
    vmem = pl.BlockSpec(memory_space=pltpu.VMEM)
    return pl.pallas_call(
        join_kernel,
        in_specs=[pl.BlockSpec(memory_space=pltpu.SMEM)] + [vmem] * 3,
        out_specs=vmem,
        out_shape=jax.ShapeDtypeStruct((2,) + own.shape, jnp.bfloat16),
        cost_estimate=pl.CostEstimate(flops=1 << 20, bytes_accessed=2 << 20, transcendentals=0),
        compiler_params=pltpu.CompilerParams(vmem_limit_bytes=SMALL),
        name="join",
    )(place, own, got, far)


def gather_weights(place, ws, ds, w_all, d_all, pick):
    rows, cols = ws[0].shape
    ff = ds[0].shape[0] // 2
    q, j = place[0], place[1]
    hidden = cols // 2
    for k, w in enumerate(ws):
        w_all[pl.ds(pl.multiple_of((q ^ k) * rows, rows), rows), :] = w[...]
    r = q % 2
    for e in range(2):
        d_all[pl.ds(pl.multiple_of((2 * e + r) * ff, ff), ff), :] = ds[0][pl.ds(e * ff, ff), :]
        d_all[pl.ds(pl.multiple_of((2 * e + 1 - r) * ff, ff), ff), :] = ds[1][pl.ds(e * ff, ff), :]
    lane = lax.broadcasted_iota(jnp.int32, (LANES, cols), 0)
    col = lax.broadcasted_iota(jnp.int32, (LANES, cols), 1)
    n = LANES // 8
    expert = 2 * j + jnp.where(col % hidden >= hidden // 2, 1, 0)
    first = jnp.where(col < hidden, expert, expert + 2 * n)
    second = jnp.where(col < hidden, expert + n, -1)
    hit = jnp.where(lane == first, 1.0, 0.0) + jnp.where(lane == second, 1.0, 0.0)
    pick[...] = hit.astype(jnp.bfloat16)


def grad_mid(xs, xo, w_all, d_all, pick, gm, gw):
    width, cols = w_all.shape
    hidden = cols // 2
    count = xs.shape[0] // 2
    for b in range(4):
        x = xs if b < 2 else xo
        at, to = pl.ds((b % 2) * count, count), pl.ds(b * count, count)
        gu = jnp.dot(x[at, :width], w_all[...], preferred_element_type=jnp.float32)
        dh = lax.dot_general(
            x[at, width : 2 * width], d_all[...], NT, preferred_element_type=jnp.float32
        )
        wm = jnp.dot(x[at, 2 * width :], pick[...], preferred_element_type=jnp.float32)
        w, on = wm[:, :hidden], wm[:, hidden:]
        gate, up = gu[:, :hidden], gu[:, hidden:]
        sg = 0.5 * jnp.tanh(0.5 * gate) + 0.5
        dhs = dh * on * sg
        gg = dhs * up * (1.0 + gate * (1.0 - sg))
        gup = dhs * gate
        gm[to, :hidden] = gg.astype(jnp.bfloat16)
        gm[to, hidden:] = gup.astype(jnp.bfloat16)
        gw[to, :hidden] = (gg * w).astype(jnp.bfloat16)
        gw[to, hidden:] = (gup * w).astype(jnp.bfloat16)


def weights_kernel(place, w0, w1, w2, w3, d0, d1, w_all, d_all, pick):
    gather_weights(place, (w0, w1, w2, w3), (d0, d1), w_all, d_all, pick)


def vmem_call(kernel, name, outs, *args, place=None, flops=HIDE):
    vmem = pl.BlockSpec(memory_space=pltpu.VMEM)
    specs = [vmem] * len(args)
    if place is not None:
        args, specs = (place, *args), [pl.BlockSpec(memory_space=pltpu.SMEM)] + specs
    return pl.pallas_call(
        kernel,
        in_specs=specs,
        out_specs=[vmem] * len(outs),
        out_shape=[jax.ShapeDtypeStruct(o, jnp.bfloat16) for o in outs],
        compiler_params=pltpu.CompilerParams(vmem_limit_bytes=VMEM),
        cost_estimate=pl.CostEstimate(flops=flops, bytes_accessed=12 << 20, transcendentals=0),
        name=name,
    )(*args)


def token_kernel(gw, w_all, ts, to):
    n = ts.shape[0]
    for b, out in enumerate((ts, to)):
        out[...] = lax.dot_general(
            gw[pl.ds(b * n, n), :], w_all[...], NT, preferred_element_type=jnp.float32
        ).astype(jnp.bfloat16)


def outer_kernel(scale, half, count, place, *refs):
    xs, gs, outs = refs[: 2 * half], refs[2 * half : 3 * half], refs[3 * half :]
    acc = None
    for k in range(half):
        x = jnp.concatenate([x[...] for x in xs[2 * k : 2 * k + 2]], 0)
        part = lax.dot_general(x, gs[k][...], TN, preferred_element_type=jnp.float32)
        acc = part if acc is None else acc + part
    value = (acc * scale).astype(jnp.bfloat16)
    for k in range(count):

        @pl.when(pl.program_id(0) == k)
        def _():
            outs[k][...] = value


def outer(place, xs, gs, scale, rows, top, count, flops=HIDE):
    cols = gs[0].shape[1]
    return pl.pallas_call(
        functools.partial(outer_kernel, scale, len(gs), count),
        grid_spec=pltpu.PrefetchScalarGridSpec(
            num_scalar_prefetch=1,
            grid=(count,),
            in_specs=[pl.BlockSpec((x.shape[0], rows), lambda i, s: (0, s[0] ^ (top - i))) for x in xs]
            + [pl.BlockSpec(g.shape, lambda i, s: (0, 0)) for g in gs],
            out_specs=[pl.BlockSpec((rows, cols), lambda i, s: (0, 0))] * count,
        ),
        out_shape=[jax.ShapeDtypeStruct((rows, cols), jnp.bfloat16)] * count,
        compiler_params=pltpu.CompilerParams(
            vmem_limit_bytes=VMEM, dimension_semantics=("arbitrary",)
        ),
        cost_estimate=pl.CostEstimate(flops=flops, bytes_accessed=12 << 20, transcendentals=0),
        name="outer",
    )(place, *xs, *gs)


def by_tokens(tokens, cotangent, expert_ids, route_weights, weight_in, weight_down):
    count, width = tokens.shape
    n_dp = lax.axis_size("dp")
    peers = lax.axis_size("expert")
    half = n_dp // 2
    rows, _, cols = weight_in.shape
    ff_rows = weight_down.shape[0]
    grad_scale = float(count * expert_ids.shape[1] * n_dp // weight_in.shape[1]) ** (-0.5)
    q = lax.axis_index("dp")
    place = jnp.stack([q, lax.axis_index("expert")]).astype(jnp.int32)
    across = [(i, (i + half) % n_dp) for i in range(n_dp)]
    beside = [(i, i ^ 1) for i in range(n_dp)]
    cores = [(i, i ^ 1) for i in range(peers)]
    hops = [[(i, i ^ (2 * m)) for i in range(peers)] for m in (1, 2, 3)]

    payload = payload_of(tokens, cotangent, expert_ids, route_weights)

    def spread(x):
        return [lax.ppermute(x, "expert", hop) for hop in hops]

    def plus(a, b):
        return (a.astype(jnp.float32) + b.astype(jnp.float32)).astype(jnp.bfloat16)

    after = lax.optimization_barrier

    near = [payload] + spread(payload)
    far_payload = lax.ppermute(payload, "dp", across)
    down1 = lax.ppermute(weight_down, "dp", beside)
    weight_in, payload = after((weight_in, payload))
    kept, given = halves(place, weight_in.swapaxes(0, 1))
    given, kept, far_payload = after((given, kept, far_payload))
    far = [far_payload] + spread(far_payload)
    w2 = lax.ppermute(given, "dp", across)
    w1 = lax.ppermute(kept, "dp", beside)
    downs = [d.swapaxes(0, 1).reshape(2 * ff_rows, width) for d in (weight_down, down1)]
    w2, w1, far[0] = after((w2, w1, far[0]))
    w3 = lax.ppermute(w2, "dp", beside)
    far_own = jnp.concatenate(far, 0)
    far_sib = lax.ppermute(far_own, "expert", cores)
    near_own = jnp.concatenate(near, 0)
    tall, wide = near_own.shape
    cols = kept.shape[1]
    mid_shape, token_shape = (2 * tall, cols), (tall, width)
    w_all, d_all, pick = vmem_call(
        weights_kernel,
        "weights",
        [(width, cols), (4 * ff_rows, width), (LANES, cols)],
        *(kept, w1, w2, w3, *downs),
        place=place,
    )
    far_sib, w_all, near_own = after((far_sib, w_all, near_own))
    near_sib = lax.ppermute(near_own, "expert", cores)

    def back_sums(own, got):
        return [plus(own[k * count : (k + 1) * count], got[k * count : (k + 1) * count]) for k in range(4)]

    def back_hops(sums):
        return [sums[0]] + [lax.ppermute(t, "expert", hop) for t, hop in zip(sums[1:], hops)]

    def mids(name, sib, own):
        return vmem_call(grad_mid, name, [mid_shape, mid_shape], sib, own, w_all, d_all, pick)

    def backs(name, gw, flops):
        return vmem_call(token_kernel, name, [token_shape] * 2, gw, w_all, flops=flops)

    far_mid, far_gw = mids("far", far_sib, far_own)
    near_sib, far_mid = after((near_sib, far_mid))
    near_mid, near_gw = mids("near", near_sib, near_own)
    tiles = (far_sib, far_own, near_sib, near_own)
    (g3,) = outer(place, tiles, (far_mid, near_mid), grad_scale, rows, 3, 1)
    got3 = lax.ppermute(g3, "dp", beside)
    far_gw, g3 = after((far_gw, g3))
    far_ts, far_to = backs("far_tokens", far_gw, 1 << 20)
    far_got = lax.ppermute(far_ts, "expert", cores)
    near_mid, far_to = after((near_mid, far_to))
    g2, g1 = outer(place, tiles, (far_mid, near_mid), grad_scale, rows, 2, 2)
    got1 = lax.ppermute(g1, "dp", beside)
    far_got, g2 = after((far_got, g2))
    far_sums = back_sums(far_to, far_got)
    far_back = back_hops(far_sums)
    got3, *far_sums = after((got3, *far_sums))
    relay = plus(g2, got3)
    away_half = lax.ppermute(relay, "dp", across)
    near_gw, relay = after((near_gw, relay))
    near_ts, near_to = backs("near_tokens", near_gw, HIDE)
    near_got = lax.ppermute(near_ts, "expert", cores)
    near_mid, near_to, *far_back = after((near_mid, near_to, *far_back))
    (g0,) = outer(place, tiles, (far_mid, near_mid), grad_scale, rows, 0, 1)
    near_got, g0 = after((near_got, g0))
    near_sums = back_sums(near_to, near_got)
    away = sum(t.astype(jnp.float32) for t in far_back).astype(jnp.bfloat16)
    away, *near_sums = after((away, *near_sums))
    home = lax.ppermute(away, "dp", across)
    near_back = back_hops(near_sums)
    grad_in = join(place, g0, got1, away_half).swapaxes(0, 1)
    near_total = sum(t.astype(jnp.float32) for t in near_back)
    near_total, home = after((near_total, home))
    token_grad = (near_total + home.astype(jnp.float32)).astype(jnp.bfloat16)
    return token_grad, grad_in


def on_device(tokens, cotangent, expert_ids, route_weights, weight_in, weight_down):
    peers, n_dp = lax.axis_size("expert"), lax.axis_size("dp")
    experts = weight_in.shape[1] * peers
    capacity = 5 * tokens.shape[0] * expert_ids.shape[1] // (4 * experts)
    dense = weight_in.shape[1] * capacity >= tokens.shape[0]
    if dense and weight_in.shape[1] == 2 and n_dp == 4 and peers == 8 and experts == 16:
        form = by_tokens
    else:
        form = by_routes
    return form(tokens, cotangent, expert_ids, route_weights, weight_in, weight_down)


def solution(mesh):
    placed = (
        P(("dp", "expert"), None),
        P(("dp", "expert"), None),
        P(("dp", "expert"), None),
        P(("dp", "expert"), None),
        P("dp", "expert", None),
        P("dp", "expert", None),
    )
    return jax.shard_map(
        on_device,
        mesh=mesh,
        in_specs=placed,
        out_specs=(P(("dp", "expert"), None), P("dp", "expert", None)),
        check_vma=False,
    )
```
